128 devices in a mesh: snap: 8 (over x, core), node: 16 (over z, y).
Axes of the slice: x: 4, y: 4, z: 4, core: 2. Of those that a mesh axis runs over, the one named last changes fastest.
Arguments:
- features: bfloat16 [8, 16384, 256], P('snap', 'node'), may hold values from -6 to 6
- tile_ids: int32 [8, 128, 4], P('snap', 'node'), may hold values from 0 to 23
- tile_values: bfloat16 [8, 128, 4, 128, 128], P('snap', 'node'), may hold values from -0.25 to 0.25
- pos_edges: int32 [8, 2, 16384], P('snap', None, 'node'), may hold values from 0 to 1023
- neg_edges: int32 [8, 2, 16384], P('snap', None, 'node'), may hold values from 0 to 1023
- initial_weight: float32 [256, 256], replicated, may hold values from -0.375 to 0.375
- gate_mats: float32 [4, 256, 256], replicated, may hold values from -0.75 to 0.75
- gate_bias: float32 [3, 256, 256], replicated, may hold values from -1.5 to 1.5
Outputs:
- snapshot_adjoint: float32 [8, 256, 256], P('snap', 'node')
- gate_grads: float32 [7, 256, 256], replicated
- initial_grad: float32 [256, 256], replicated
The draws below stay inside these ranges and needn't reach their ends.
Inputs may be any that keep to these rules, and one draw needn't show every extreme that they name: `tile_ids`: block numbers count the blocks of the device's extended rows: the 1024 rows before its first row, its own 1024 rows, then the 1024 rows after its last. `pos_edges`: node numbers within the device's own rows. `neg_edges`: node numbers within the device's own rows.
All inputs are finite; a program needn't handle non-finite values.
Results may differ from the reference program's by a relative error of at most 0.0054.
Values may be sent and summed in bfloat16 or wider, within the bound.
No kernel may reach another device: no remote copies, remote signals or barrier semaphores. Data moves between devices by JAX's collectives and lax.ppermute only.
A program may use at most 128 MiB of HBM per device.

```python
import jax
import jax.numpy as jnp
from jax import lax

F = 256
ROWS_DEV = 1024
BLOCK = 128
TILES = 4
HALO = 1024
EDGES_DEV = 1024
SNAPS = 8
ROWS = 16384
EDGES = 16384
EXT_BLOCKS = 24
BLOCKS = 128
N_NODE = 16


def place_ends(values, key, least, top_value):
    dims = values.shape
    spot = [jax.random.randint(jax.random.fold_in(key, axis), (), 0, dims[axis]) for axis in range(len(dims))]
    values = values.at[tuple(spot)].set(least)
    longest = dims.index(max(dims))
    spot[longest] = (spot[longest] + 1) % dims[longest]
    return values.at[tuple(spot)].set(top_value)


def level_of(own_key, extent, cuts, low, largest):
    factor_of = 1.0
    for position, shards_of in cuts:
        draws = jax.random.uniform(jax.random.fold_in(jax.random.fold_in(own_key, 6), position), (shards_of,), jnp.float32, low / len(cuts), largest / len(cuts))
        factor_of = factor_of * jnp.repeat(jnp.exp(draws), extent[position] // shards_of).reshape((-1,) + (1,) * (len(extent) - 1 - position))
    return factor_of


def scatter_about(own_key, extent, scale, reach, split=(), kind=jnp.bfloat16):
    drawn = scale * jax.random.normal(own_key, extent, jnp.float32)
    if split:
        drawn = drawn * level_of(own_key, extent, split, -0.22, 0.18)
    return jnp.clip(drawn, -reach, reach).astype(kind)


def setup_inputs(seed: int = 0) -> dict:
    key_of = jax.random.split(jax.random.key(seed), 9)
    features = scatter_about(key_of[0], (SNAPS, ROWS, F), 1.0, 6.0, ((0, 8), (1, 16)))
    tile_ids = place_ends(jax.random.randint(key_of[1], (SNAPS, BLOCKS, TILES), 0, EXT_BLOCKS), jax.random.fold_in(key_of[1], 1), 0, EXT_BLOCKS - 1).astype(jnp.int32)
    tile_values = scatter_about(key_of[2], (SNAPS, BLOCKS, TILES, BLOCK, BLOCK), (TILES * BLOCK) ** -0.5, 0.25, ((0, 8), (1, 16)))
    pos_edges = place_ends(jax.random.randint(key_of[3], (SNAPS, 2, EDGES), 0, ROWS_DEV), jax.random.fold_in(key_of[3], 1), 0, ROWS_DEV - 1).astype(jnp.int32)
    neg_edges = place_ends(jax.random.randint(key_of[4], (SNAPS, 2, EDGES), 0, ROWS_DEV), jax.random.fold_in(key_of[4], 1), 0, ROWS_DEV - 1).astype(jnp.int32)
    initial_weight = scatter_about(key_of[5], (F, F), F ** -0.5, 0.375, (), jnp.float32)
    gate_mats = scatter_about(key_of[6], (4, F, F), (F // 4) ** -0.5, 0.75, (), jnp.float32)
    gate_bias = scatter_about(key_of[7], (3, F, F), 0.25, 1.5, (), jnp.float32)
    return {"features": features, "tile_ids": tile_ids, "tile_values": tile_values, "pos_edges": pos_edges, "neg_edges": neg_edges, "initial_weight": initial_weight, "gate_mats": gate_mats, "gate_bias": gate_bias}


def evolve(weight, gate_mats, gate_bias):
    best = lax.Precision.HIGHEST
    update = jax.nn.sigmoid(jnp.dot(gate_mats[0], weight, preferred_element_type=jnp.float32, precision=best) + gate_bias[0])
    reset = jax.nn.sigmoid(jnp.dot(gate_mats[1], weight, preferred_element_type=jnp.float32, precision=best) + gate_bias[1])
    inner = jnp.dot(gate_mats[2], weight, preferred_element_type=jnp.float32, precision=best)
    inner = inner + jnp.dot(gate_mats[3], reset * weight, preferred_element_type=jnp.float32, precision=best)
    proposal = jnp.tanh(inner + gate_bias[2])
    return (1.0 - update) * weight + update * proposal

def edge_terms(embed, pairs, sign, factor):
    left = embed[pairs[0]]
    right = embed[pairs[1]]
    score = lax.optimization_barrier(jnp.sum(left * right, axis=1)) / embed.shape[1]
    slope = -sign * jax.nn.sigmoid(-sign * score) * factor
    total = embed.shape[0]
    first = jax.ops.segment_sum(slope[:, None] * right, pairs[0], num_segments=total)
    second = jax.ops.segment_sum(slope[:, None] * left, pairs[1], num_segments=total)
    return first + second

def aggregate(features_t, ids_t, values_t):
    padded = jnp.pad(features_t, ((HALO, HALO), (0, 0)))
    per_dev = ROWS_DEV // BLOCK

    def one_device(index):
        start = (index * ROWS_DEV).astype(jnp.int32)
        extended = lax.dynamic_slice_in_dim(padded, start, ROWS_DEV + 2 * HALO, 0).reshape(-1, BLOCK, F)
        bstart = (index * per_dev).astype(jnp.int32)
        ids = lax.dynamic_slice_in_dim(ids_t, bstart, per_dev, 0)
        values = lax.dynamic_slice_in_dim(values_t, bstart, per_dev, 0)
        sources = extended[ids]
        summed = jnp.einsum('nkab,nkbf->naf', values.astype(jnp.float32), sources.astype(jnp.float32))
        return summed.reshape(ROWS_DEV, F).astype(jnp.bfloat16)
    return lax.map(one_device, jnp.arange(N_NODE, dtype=jnp.int32)).reshape(ROWS, F)

def reference(features, tile_ids, tile_values, pos_edges, neg_edges, initial_weight, gate_mats, gate_bias):
    factor = float(ROWS) ** (-0.5)
    befores = []
    weights = []
    current = initial_weight
    for snap_step in range(SNAPS):
        befores.append(current)
        current = evolve(current, gate_mats, gate_bias)
        weights.append(current)
    offsets = jnp.arange(EDGES, dtype=jnp.int32) // EDGES_DEV * ROWS_DEV
    grads = []
    for snap_step in range(SNAPS):
        aggregated = aggregate(features[snap_step], tile_ids[snap_step], tile_values[snap_step])
        embed = jnp.dot(aggregated, weights[snap_step].astype(jnp.bfloat16), preferred_element_type=jnp.float32)
        positive = pos_edges[snap_step] + offsets[None, :]
        negative = neg_edges[snap_step] + offsets[None, :]
        embed_grad = (edge_terms(embed, positive, 1.0, factor) + edge_terms(embed, negative, -1.0, factor)).astype(jnp.bfloat16)
        grads.append(lax.dot_general(aggregated, embed_grad, (((0,), (0,)), ((), ())), preferred_element_type=jnp.float32))
    carry = jnp.zeros((F, F), jnp.float32)
    mat_total = jnp.zeros((4, F, F), jnp.float32)
    bias_total = jnp.zeros((3, F, F), jnp.float32)
    adjoints = [None] * SNAPS
    for snap_step in reversed(range(SNAPS)):
        adjoint = grads[snap_step] + carry
        adjoints[snap_step] = adjoint
        unused, pullback = jax.vjp(evolve, befores[snap_step], gate_mats, gate_bias)
        carry, mat_part, bias_part = pullback(adjoint)
        mat_total = mat_total + mat_part
        bias_total = bias_total + bias_part
    return (jnp.stack(adjoints), jnp.concatenate([mat_total, bias_total], axis=0), carry)
```

```python
import functools

import jax
import jax.numpy as jnp
from jax import lax
from jax.experimental import pallas as pl
from jax.experimental.pallas import tpu as pltpu
from jax.sharding import PartitionSpec as P

HALO = 1024
RING = 4
PACK_EXTRA = 16
F32 = jnp.float32
BF16 = jnp.bfloat16
INNER = (((1,), (0,)), ((), ()))
LANES = (((1,), (1,)), ((), ()))
ROWS = (((0,), (0,)), ((), ()))


def split(value):
    high = value.astype(BF16)
    return high, (value - high.astype(F32)).astype(BF16)


def dot(left, right, dims=INNER):
    return lax.dot_general(left, right, dims, preferred_element_type=F32)


def dot3(left, right, dims=INNER):
    return (
        dot(left[0], right[0], dims) + dot(left[0], right[1], dims) + dot(left[1], right[0], dims)
    )


def sigmoid(value):
    return 0.5 * jnp.tanh(0.5 * value) + 0.5


def forward_kernel(start, mats, bias, before, update, reset, proposal, low, mats_high, mats_low):
    steps = low.shape[0]
    width = start.shape[0]
    for k in range(4):
        high, rest = split(mats[k])
        mats_high[pl.ds(k * width, width), :] = high
        mats_low[pl.ds(k * width, width), :] = rest
    before[0] = start[...]

    def step(t, carry):
        weight = before[t]
        parts = split(weight)
        top = pl.ds(0, 3 * width)
        gates = dot3((mats_high[top, :], mats_low[top, :]), parts)
        r = sigmoid(gates[width : 2 * width] + bias[1])
        last = pl.ds(3 * width, width)
        inner = gates[2 * width :] + dot3((mats_high[last, :], mats_low[last, :]), split(r * weight))
        u = sigmoid(gates[:width] + bias[0])
        c = jnp.tanh(inner + bias[2])
        fresh = (1.0 - u) * weight + u * c
        update[t] = u
        reset[t] = r
        proposal[t] = c
        low[t] = fresh.astype(BF16)

        @pl.when(t + 1 < steps)
        def _():
            before[t + 1] = fresh

        return carry

    lax.fori_loop(0, steps, step, 0)


def edge_kernel(
    factor, where, ids, own, left, right, tiles, columns, low, packed, extended, aggregated, picked
):
    rows, width = own.shape
    side = tiles.shape[1]
    blocks = rows // side
    per_block = ids.shape[1]
    extended[pl.ds(0, blocks)] = left[...].reshape(blocks, side, width)
    extended[pl.ds(blocks, blocks)] = own[...].reshape(blocks, side, width)
    extended[pl.ds(2 * blocks, blocks)] = right[...].reshape(blocks, side, width)
    for b in range(blocks):
        total = jnp.zeros((side, width), F32)
        for k in range(per_block):
            total = total + dot(tiles[b * per_block + k], extended[ids[b, k]])
        aggregated[pl.ds(b * side, side), :] = total.astype(BF16)

    count = columns.shape[0]
    chunk = 512
    for c in range(count // chunk):
        index = columns[pl.ds(c * chunk, chunk), :]
        lane = lax.broadcasted_iota(jnp.int32, (chunk, rows), 1)
        onehot = (lane == index).astype(F32).astype(BF16)
        picked[pl.ds(c * chunk, chunk), :] = dot(onehot, aggregated[...]).astype(BF16)

    weight_low = low[where[0]]
    edges = count // 4
    half = jnp.zeros((width, width), F32)
    for sign in (0, 1):
        first = picked[pl.ds(2 * sign * edges, edges), :]
        second = picked[pl.ds((2 * sign + 1) * edges, edges), :]
        ends = dot(first, weight_low) * dot(second, weight_low)
        score = jnp.sum(ends, axis=1, keepdims=True) * (1.0 / width)
        if sign == 0:
            slope = sigmoid(-score) * (-factor)
        else:
            slope = sigmoid(score) * factor
        scaled = split(slope * first.astype(F32))
        half = half + dot(scaled[0], second, ROWS) + dot(scaled[1], second, ROWS)
    full = half + half.T
    quarter = width // 2
    upper = full[:quarter, :quarter]
    lower = full[quarter:, quarter:]
    i = lax.broadcasted_iota(jnp.int32, (quarter, quarter), 0)
    j = lax.broadcasted_iota(jnp.int32, (quarter, quarter), 1)
    diagonal = jnp.sum(jnp.where(i == j, lower, 0.0), axis=0, keepdims=True)
    packed[pl.ds(0, quarter), :] = full[:quarter, quarter:].astype(BF16)
    packed[pl.ds(quarter, quarter), :] = jnp.where(i <= j, upper, lower).astype(BF16)
    packed[pl.ds(2 * quarter, PACK_EXTRA), :] = jnp.broadcast_to(
        diagonal, (PACK_EXTRA, quarter)
    ).astype(BF16)


def backward_kernel(
    where,
    pieces,
    before,
    update,
    reset,
    proposal,
    low,
    mats_high,
    mats_low,
    adjoint_rows,
    grads,
    initial_grad,
    flipped_high,
    flipped_low,
    local,
    adjoints,
):
    steps, width = low.shape[0], low.shape[1]
    quarter = width // 2
    x, core, node = where[0], where[1], where[2]
    for k in range(4):
        area = pl.ds(k * width, width)
        flipped_high[k] = mats_high[area, :].T
        flipped_low[k] = mats_low[area, :].T
    i = lax.broadcasted_iota(jnp.int32, (quarter, quarter), 0)
    j = lax.broadcasted_iota(jnp.int32, (quarter, quarter), 1)
    for t in range(steps):
        side = lax.rem(core + t % 2, 2)
        turn = lax.rem(x - t // 2 + RING, RING)
        piece = pieces[side, turn]
        corner = piece[:quarter]
        mixed = piece[quarter : 2 * quarter].astype(F32)
        diagonal = piece[2 * quarter :].astype(F32)[0:1]
        turned = mixed.T
        upper = jnp.where(i <= j, mixed, turned).astype(BF16)
        lower = jnp.where(i > j, mixed, jnp.where(i < j, turned, diagonal)).astype(BF16)
        weight = low[t]
        top, bottom = weight[:quarter], weight[quarter:]
        local[t, pl.ds(0, quarter), :] = dot(upper, top) + dot(corner, bottom)
        local[t, pl.ds(quarter, quarter), :] = dot(corner.T, top) + dot(lower, bottom)

    grads[...] = jnp.zeros_like(grads)

    def step(s, carry):
        t = steps - 1 - s
        g = local[t] + carry
        adjoints[t] = g
        weight, u, r, c = before[t], update[t], reset[t], proposal[t]
        keep = 1.0 - u
        d0 = g * (c - weight) * (u * keep)
        d2 = g * u * (1.0 - c * c)
        d2_parts = split(d2)
        inner = dot3((flipped_high[3], flipped_low[3]), d2_parts)
        d0_parts = split(d0)
        d1 = inner * weight * (r * (1.0 - r))
        d1_parts = split(d1)
        fresh = g * keep + inner * r
        fresh = fresh + dot3((flipped_high[0], flipped_low[0]), d0_parts)
        fresh = fresh + dot3((flipped_high[2], flipped_low[2]), d2_parts)
        fresh = fresh + dot3((flipped_high[1], flipped_low[1]), d1_parts)
        weight_parts = split(weight)
        grads[0] += dot3(d0_parts, weight_parts, LANES)
        grads[1] += dot3(d1_parts, weight_parts, LANES)
        grads[2] += dot3(d2_parts, weight_parts, LANES)
        grads[3] += dot3(d2_parts, split(r * weight), LANES)
        grads[4] += d0
        grads[5] += d1
        grads[6] += d2
        return fresh

    initial_grad[...] = lax.fori_loop(0, steps, step, jnp.zeros((width, width), F32))
    share = adjoint_rows.shape[0]
    start = pl.multiple_of(node * share, share)
    adjoint_rows[...] = adjoints[2 * x + core, pl.ds(start, share), :]


def params(megabytes):
    return pltpu.CompilerParams(vmem_limit_bytes=megabytes * 2**20)


VMEM = pl.BlockSpec(memory_space=pltpu.VMEM)
SMEM = pl.BlockSpec(memory_space=pltpu.SMEM)


def ring_parts(block, axis, stride, count):
    size = lax.axis_size(axis)
    span = stride * count
    parts = []
    for turn in range(1, count):
        route = [
            (i, i - i % span + (i % span + turn * stride) % span) for i in range(size)
        ]
        parts.append(lax.ppermute(block, axis, route))
    return parts


def ring_sum(block, axis, stride, count):
    parts = ring_parts(block, axis, stride, count)
    total = block.astype(F32)
    for part in parts:
        total = total + part.astype(F32)
    return total.astype(BF16)


def body(
    features, tile_ids, tile_values, pos_edges, neg_edges, initial_weight, gate_mats, gate_bias
):
    snap_count = lax.axis_size("snap")
    node_count = lax.axis_size("node")
    place = lax.axis_index("snap")
    node = lax.axis_index("node")
    own = features[0]
    rows, width = own.shape
    side = tile_values.shape[-1]
    per_block = tile_ids.shape[-1]
    square = (snap_count, width, width)

    ends = node_count - 1
    left = lax.ppermute(own[rows - HALO :], "node", [(i, i + 1) for i in range(ends)])
    right = lax.ppermute(own[:HALO], "node", [(i + 1, i) for i in range(ends)])

    wide = jax.ShapeDtypeStruct(square, F32)
    tall = jax.ShapeDtypeStruct((4 * width, width), BF16)
    before, update, reset, proposal, low, mats_high, mats_low = pl.pallas_call(
        forward_kernel,
        out_shape=[wide, wide, wide, wide, jax.ShapeDtypeStruct(square, BF16), tall, tall],
        in_specs=[VMEM] * 3,
        out_specs=[VMEM] * 7,
        compiler_params=params(32),
        name="forward_chain",
    )(initial_weight, gate_mats, gate_bias)

    columns = jnp.concatenate(
        [pos_edges[0, 0], pos_edges[0, 1], neg_edges[0, 0], neg_edges[0, 1]]
    ).reshape(-1, 1)
    factor = float(rows * node_count) ** (-0.5)
    pack_rows = width + PACK_EXTRA
    packed = pl.pallas_call(
        functools.partial(edge_kernel, factor),
        out_shape=jax.ShapeDtypeStruct((pack_rows, width // 2), BF16),
        in_specs=[SMEM, SMEM] + [VMEM] * 6,
        out_specs=VMEM,
        scratch_shapes=[
            pltpu.VMEM(((rows + 2 * HALO) // side, side, width), BF16),
            pltpu.VMEM((rows, width), BF16),
            pltpu.VMEM((columns.shape[0], width), BF16),
        ],
        compiler_params=params(40),
        name="edge_products",
    )(
        jnp.stack([place, node]),
        tile_ids[0],
        own,
        left,
        right,
        tile_values.reshape(-1, side, side),
        columns,
        low,
    )

    packed = ring_sum(packed, "node", 1, RING)
    packed = ring_sum(packed, "node", RING, node_count // RING)
    along = jnp.stack([packed] + ring_parts(packed, "snap", 2, snap_count // 2))
    other = lax.ppermute(along, "snap", [(i, i ^ 1) for i in range(snap_count)])
    pieces = jnp.stack([along, other])

    share = width // node_count
    adjoint_rows, grads, initial_grad = pl.pallas_call(
        backward_kernel,
        out_shape=[
            jax.ShapeDtypeStruct((share, width), F32),
            jax.ShapeDtypeStruct((7, width, width), F32),
            jax.ShapeDtypeStruct((width, width), F32),
        ],
        in_specs=[SMEM] + [VMEM] * 8,
        out_specs=[VMEM] * 3,
        scratch_shapes=[
            pltpu.VMEM((4, width, width), BF16),
            pltpu.VMEM((4, width, width), BF16),
            pltpu.VMEM(square, F32),
            pltpu.VMEM(square, F32),
        ],
        compiler_params=params(40),
        name="backward_chain",
    )(
        jnp.stack([place // 2, place % 2, node]),
        pieces,
        before,
        update,
        reset,
        proposal,
        low,
        mats_high,
        mats_low,
    )
    return adjoint_rows[None], grads, initial_grad


def solution(mesh):
    placed = (
        P("snap", "node", None),
        P("snap", "node", None),
        P("snap", "node", None, None, None),
        P("snap", None, "node"),
        P("snap", None, "node"),
        P(),
        P(),
        P(),
    )
    return jax.shard_map(
        body,
        mesh=mesh,
        in_specs=placed,
        out_specs=(P("snap", "node", None), P(), P()),
        check_vma=False,
    )
```

```python
import functools

import jax
import jax.numpy as jnp
from jax import lax
from jax.experimental import pallas as pl
from jax.experimental.pallas import tpu as pltpu
from jax.sharding import PartitionSpec as P

HALO = 1024
RING = 4
PACK_EXTRA = 16
F32 = jnp.float32
BF16 = jnp.bfloat16
INNER = (((1,), (0,)), ((), ()))
LANES = (((1,), (1,)), ((), ()))
ROWS = (((0,), (0,)), ((), ()))


def split(value):
    high = value.astype(BF16)
    return high, (value - high.astype(F32)).astype(BF16)


def dot(left, right, dims=INNER):
    return lax.dot_general(left, right, dims, preferred_element_type=F32)


def dot3(left, right, dims=INNER):
    return (
        dot(left[0], right[0], dims) + dot(left[0], right[1], dims) + dot(left[1], right[0], dims)
    )


def sigmoid(value):
    return 0.5 * jnp.tanh(0.5 * value) + 0.5


def forward_kernel(start, mats, bias, before, update, reset, proposal, low, mats_high, mats_low):
    steps = low.shape[0]
    width = start.shape[0]
    for k in range(4):
        high, rest = split(mats[k])
        mats_high[pl.ds(k * width, width), :] = high
        mats_low[pl.ds(k * width, width), :] = rest
    before[0] = start[...]

    def step(t, carry):
        weight = before[t]
        parts = split(weight)
        top = pl.ds(0, 3 * width)
        gates = dot3((mats_high[top, :], mats_low[top, :]), parts)
        r = sigmoid(gates[width : 2 * width] + bias[1])
        last = pl.ds(3 * width, width)
        inner = gates[2 * width :] + dot3((mats_high[last, :], mats_low[last, :]), split(r * weight))
        u = sigmoid(gates[:width] + bias[0])
        c = jnp.tanh(inner + bias[2])
        fresh = (1.0 - u) * weight + u * c
        update[t] = u
        reset[t] = r
        proposal[t] = c
        low[t] = fresh.astype(BF16)

        @pl.when(t + 1 < steps)
        def _():
            before[t + 1] = fresh

        return carry

    lax.fori_loop(0, steps, step, 0)


def edge_kernel(
    factor,
    ids,
    own,
    left,
    right,
    tiles,
    pos,
    neg,
    low,
    first_out,
    second_out,
    third_out,
    extended,
    aggregated,
    picked,
):
    rows, width = own.shape
    side = tiles.shape[1]
    blocks = rows // side
    per_block = ids.shape[1]
    extended[pl.ds(0, blocks)] = left[...].reshape(blocks, side, width)
    extended[pl.ds(blocks, blocks)] = own[...].reshape(blocks, side, width)
    extended[pl.ds(2 * blocks, blocks)] = right[...].reshape(blocks, side, width)
    for b in range(blocks):
        total = jnp.zeros((side, width), F32)
        for k in range(per_block):
            total = total + dot(tiles[b * per_block + k], extended[ids[b, k]])
        aggregated[pl.ds(b * side, side), :] = total.astype(BF16)

    edges = pos.shape[1]
    chunk = 512
    lane = lax.broadcasted_iota(jnp.int32, (chunk, side), 1)
    for c in range(4 * edges // chunk):
        end, offset = divmod(c * chunk, edges)
        source = (pos, neg)[end // 2]
        turned = [
            jnp.broadcast_to(
                source[pl.ds(end % 2, 1), pl.ds(offset + part * side, side)], (side, side)
            ).T
            for part in range(chunk // side)
        ]
        index = jnp.concatenate(turned, axis=0)
        onehot = jnp.concatenate(
            [(index == lane + part * side).astype(F32).astype(BF16) for part in range(rows // side)],
            axis=1,
        )
        picked[pl.ds(c * chunk, chunk), :] = dot(onehot, aggregated[...]).astype(BF16)

    weight_low = low[lax.axis_index("snap")]
    half = jnp.zeros((width, width), F32)
    for sign in (0, 1):
        first = picked[pl.ds(2 * sign * edges, edges), :]
        second = picked[pl.ds((2 * sign + 1) * edges, edges), :]
        ends = dot(first, weight_low) * dot(second, weight_low)
        score = jnp.sum(ends, axis=1, keepdims=True) * (1.0 / width)
        if sign == 0:
            slope = sigmoid(-score) * (-factor)
        else:
            slope = sigmoid(score) * factor
        scaled = split(slope * first.astype(F32))
        half = half + dot(scaled[0], second, ROWS) + dot(scaled[1], second, ROWS)
    full = half + half.T
    quarter = width // 2
    upper = full[:quarter, :quarter]
    lower = full[quarter:, quarter:]
    i = lax.broadcasted_iota(jnp.int32, (quarter, quarter), 0)
    j = lax.broadcasted_iota(jnp.int32, (quarter, quarter), 1)
    diagonal = jnp.sum(jnp.where(i == j, lower, 0.0), axis=0, keepdims=True)
    corner = full[:quarter, quarter:].astype(BF16)
    mixed = jnp.where(i <= j, upper, lower).astype(BF16)
    extra = jnp.broadcast_to(diagonal, (PACK_EXTRA, quarter)).astype(BF16)
    for packed in (first_out, second_out, third_out):
        packed[pl.ds(0, quarter), :] = corner
        packed[pl.ds(quarter, quarter), :] = mixed
        packed[pl.ds(2 * quarter, PACK_EXTRA), :] = extra


def backward_kernel(
    along,
    other,
    before,
    update,
    reset,
    proposal,
    low,
    mats_high,
    mats_low,
    adjoint_rows,
    grads,
    initial_grad,
    flipped_high,
    flipped_low,
    local,
    adjoints,
):
    steps, width = low.shape[0], low.shape[1]
    quarter = width // 2
    place, node = lax.axis_index("snap"), lax.axis_index("node")
    x, core = lax.div(place, 2), lax.rem(place, 2)
    for k in range(4):
        area = pl.ds(k * width, width)
        flipped_high[k] = mats_high[area, :].T
        flipped_low[k] = mats_low[area, :].T
    i = lax.broadcasted_iota(jnp.int32, (quarter, quarter), 0)
    j = lax.broadcasted_iota(jnp.int32, (quarter, quarter), 1)
    for t in range(steps):
        turn = lax.rem(x - t // 2 + RING, RING)
        piece = jnp.where(core == t % 2, along[turn], other[turn])
        corner = piece[:quarter]
        mixed = piece[quarter : 2 * quarter].astype(F32)
        diagonal = piece[2 * quarter :].astype(F32)[0:1]
        turned = mixed.T
        upper = jnp.where(i <= j, mixed, turned).astype(BF16)
        lower = jnp.where(i > j, mixed, jnp.where(i < j, turned, diagonal)).astype(BF16)
        weight = low[t]
        top, bottom = weight[:quarter], weight[quarter:]
        local[t, pl.ds(0, quarter), :] = dot(upper, top) + dot(corner, bottom)
        local[t, pl.ds(quarter, quarter), :] = dot(corner.T, top) + dot(lower, bottom)

    grads[...] = jnp.zeros_like(grads)

    def step(s, carry):
        t = steps - 1 - s
        g = local[t] + carry
        adjoints[t] = g
        weight, u, r, c = before[t], update[t], reset[t], proposal[t]
        keep = 1.0 - u
        d0 = g * (c - weight) * (u * keep)
        d2 = g * u * (1.0 - c * c)
        d2_parts = split(d2)
        inner = dot3((flipped_high[3], flipped_low[3]), d2_parts)
        d0_parts = split(d0)
        d1 = inner * weight * (r * (1.0 - r))
        d1_parts = split(d1)
        fresh = g * keep + inner * r
        fresh = fresh + dot3((flipped_high[0], flipped_low[0]), d0_parts)
        fresh = fresh + dot3((flipped_high[2], flipped_low[2]), d2_parts)
        fresh = fresh + dot3((flipped_high[1], flipped_low[1]), d1_parts)
        weight_high = weight.astype(BF16)
        grads[0] += dot(d0_parts[0], weight_high, LANES)
        grads[1] += dot(d1_parts[0], weight_high, LANES)
        grads[2] += dot(d2_parts[0], weight_high, LANES)
        grads[3] += dot(d2_parts[0], (r * weight).astype(BF16), LANES)
        grads[4] += d0
        grads[5] += d1
        grads[6] += d2
        return fresh

    initial_grad[...] = lax.fori_loop(0, steps, step, jnp.zeros((width, width), F32))
    share = adjoint_rows.shape[0]
    start = pl.multiple_of(node * share, share)
    adjoint_rows[...] = adjoints[place, pl.ds(start, share), :]


def params(megabytes):
    return pltpu.CompilerParams(vmem_limit_bytes=megabytes * 2**20)


VMEM = pl.BlockSpec(memory_space=pltpu.VMEM)
SMEM = pl.BlockSpec(memory_space=pltpu.SMEM)


def ring_parts(copies, axis, stride, count):
    size = lax.axis_size(axis)
    span = stride * count
    parts = []
    for turn in range(1, count):
        route = [(i, i - i % span + (i % span + turn * stride) % span) for i in range(size)]
        parts.append(lax.ppermute(copies[turn - 1], axis, route))
    return parts


def sum_kernel(own, first, second, third, *copies):
    total = (own[...].astype(F32) + first[...].astype(F32)) + (
        second[...].astype(F32) + third[...].astype(F32)
    )
    total = total.astype(BF16)
    for copy in copies:
        copy[...] = total


def ring_sum(copies, axis, stride, count):
    parts = ring_parts(copies, axis, stride, count)
    like = jax.ShapeDtypeStruct(copies[0].shape, BF16)
    return pl.pallas_call(
        sum_kernel,
        out_shape=[like] * 3,
        in_specs=[VMEM] * 4,
        out_specs=[VMEM] * 3,
        compiler_params=params(4),
        name="ring_sum",
    )(copies[0], *parts)


def body(
    features, tile_ids, tile_values, pos_edges, neg_edges, initial_weight, gate_mats, gate_bias
):
    snap_count = lax.axis_size("snap")
    node_count = lax.axis_size("node")
    own = features[0]
    rows, width = own.shape
    side = tile_values.shape[-1]
    square = (snap_count, width, width)

    ends = node_count - 1
    left = lax.ppermute(own[rows - HALO :], "node", [(i, i + 1) for i in range(ends)])
    right = lax.ppermute(own[:HALO], "node", [(i + 1, i) for i in range(ends)])

    wide = jax.ShapeDtypeStruct(square, F32)
    tall = jax.ShapeDtypeStruct((4 * width, width), BF16)
    before, update, reset, proposal, low, mats_high, mats_low = pl.pallas_call(
        forward_kernel,
        out_shape=[wide, wide, wide, wide, jax.ShapeDtypeStruct(square, BF16), tall, tall],
        in_specs=[VMEM] * 3,
        out_specs=[VMEM] * 7,
        compiler_params=params(16),
        name="forward_chain",
    )(initial_weight, gate_mats, gate_bias)

    factor = float(rows * node_count) ** (-0.5)
    pack_rows = width + PACK_EXTRA
    copies = pl.pallas_call(
        functools.partial(edge_kernel, factor),
        out_shape=[jax.ShapeDtypeStruct((pack_rows, width // 2), BF16)] * 3,
        in_specs=[SMEM] + [VMEM] * 7,
        out_specs=[VMEM] * 3,
        scratch_shapes=[
            pltpu.VMEM(((rows + 2 * HALO) // side, side, width), BF16),
            pltpu.VMEM((rows, width), BF16),
            pltpu.VMEM((4 * pos_edges.shape[-1], width), BF16),
        ],
        compiler_params=params(16),
        name="edge_products",
    )(
        tile_ids[0],
        own,
        left,
        right,
        tile_values.reshape(-1, side, side),
        pos_edges[0],
        neg_edges[0],
        low,
    )

    copies = ring_sum(copies, "node", 1, RING)
    copies = ring_sum(copies, "node", RING, node_count // RING)
    along = jnp.stack([copies[0]] + ring_parts(copies, "snap", 2, snap_count // 2))
    other = lax.ppermute(along, "snap", [(i, i ^ 1) for i in range(snap_count)])

    share = width // node_count
    adjoint_rows, grads, initial_grad = pl.pallas_call(
        backward_kernel,
        out_shape=[
            jax.ShapeDtypeStruct((share, width), F32),
            jax.ShapeDtypeStruct((7, width, width), F32),
            jax.ShapeDtypeStruct((width, width), F32),
        ],
        in_specs=[VMEM] * 9,
        out_specs=[VMEM] * 3,
        scratch_shapes=[
            pltpu.VMEM((4, width, width), BF16),
            pltpu.VMEM((4, width, width), BF16),
            pltpu.VMEM(square, F32),
            pltpu.VMEM(square, F32),
        ],
        compiler_params=params(16),
        name="backward_chain",
    )(
        along,
        other,
        before,
        update,
        reset,
        proposal,
        low,
        mats_high,
        mats_low,
    )
    return adjoint_rows[None], grads, initial_grad


def solution(mesh):
    placed = (
        P("snap", "node", None),
        P("snap", "node", None),
        P("snap", "node", None, None, None),
        P("snap", None, "node"),
        P("snap", None, "node"),
        P(),
        P(),
        P(),
    )
    return jax.shard_map(
        body,
        mesh=mesh,
        in_specs=placed,
        out_specs=(P("snap", "node", None), P(), P()),
        check_vma=False,
    )
```

```python
import functools

import jax
import jax.numpy as jnp
from jax import lax
from jax.experimental import pallas as pl
from jax.experimental.pallas import tpu as pltpu
from jax.sharding import PartitionSpec as P

HALO = 1024
RING = 4
PACK_EXTRA = 16
F32 = jnp.float32
BF16 = jnp.bfloat16
INNER = (((1,), (0,)), ((), ()))
LANES = (((1,), (1,)), ((), ()))
ROWS = (((0,), (0,)), ((), ()))


def split(value):
    high = value.astype(BF16)
    return high, (value - high.astype(F32)).astype(BF16)


def dot(left, right, dims=INNER):
    return lax.dot_general(left, right, dims, preferred_element_type=F32)


def dot3(left, right, dims=INNER):
    return (
        dot(left[0], right[0], dims) + dot(left[0], right[1], dims) + dot(left[1], right[0], dims)
    )


def sigmoid(value):
    return 0.5 * jnp.tanh(0.5 * value) + 0.5


def forward_kernel(
    start_hbm,
    mats_hbm,
    bias_hbm,
    keep,
    gate_slope,
    proposal_slope,
    reset_slope,
    reset,
    low,
    weights_wide,
    reset_wide,
    turned_high,
    turned_low,
    score_matrix,
    start,
    mats,
    bias,
    mats_high,
    mats_low,
    sems,
):
    steps, width = low.shape[0], low.shape[1]
    copies = [pltpu.make_async_copy(start_hbm, start, sems.at[0])]
    copies += [
        pltpu.make_async_copy(mats_hbm.at[k], mats.at[k], sems.at[1 + k]) for k in range(4)
    ]
    copies += [
        pltpu.make_async_copy(bias_hbm.at[k], bias.at[k], sems.at[5 + k]) for k in range(3)
    ]
    for copy in copies:
        copy.start()
    for copy in copies[:5]:
        copy.wait()
    for k in range(4):
        mats_high[k], mats_low[k] = split(mats[k])
    for copy in copies[5:]:
        copy.wait()

    def gate(k, parts):
        return dot3((mats_high[k], mats_low[k]), parts)

    weight = start[...]
    for t in range(steps):
        parts = split(weight)
        r = sigmoid(gate(1, parts) + bias[1])
        mixed = r * weight
        mixed_parts = split(mixed)
        u_in = gate(0, parts)
        c_in = gate(2, parts)
        u = sigmoid(u_in + bias[0])
        c = jnp.tanh(c_in + gate(3, mixed_parts) + bias[2])
        rest = 1.0 - u
        keep[t] = rest
        reset[t] = r
        gate_slope[t] = (c - weight) * (u * rest)
        proposal_slope[t] = u * (1.0 - c * c)
        reset_slope[t] = mixed * (1.0 - r)
        lanes = pl.ds(t * width, width)
        weights_wide[:, lanes] = parts[0]
        reset_wide[:, lanes] = mixed_parts[0]
        weight = rest * weight + u * c
        low[t] = weight.astype(BF16)
    for k in range(4):
        turned_high[k] = mats_high[k].T
        turned_low[k] = mats_low[k].T
    own = low[lax.axis_index("snap")]
    score_matrix[...] = dot(own, own, LANES).astype(BF16)


def edge_kernel(
    factor,
    ids,
    own,
    even_side,
    odd_side,
    tiles,
    pos,
    neg,
    score_matrix,
    *refs,
):
    *outs, extended, aggregated, picked = refs
    rows, width = own.shape
    side = tiles.shape[1]
    blocks = rows // side
    per_block = ids.shape[1]
    node, ends = lax.axis_index("node"), lax.axis_size("node") - 1
    odd = lax.rem(node, 2)
    inside = (node > 0) & (node < ends)
    far = jnp.where(inside, odd_side[...], jnp.zeros_like(odd_side))
    extended[pl.ds(2 * blocks * (1 - odd), blocks)] = even_side[...].reshape(blocks, side, width)
    extended[pl.ds(blocks, blocks)] = own[...].reshape(blocks, side, width)
    extended[pl.ds(2 * blocks * odd, blocks)] = far.reshape(blocks, side, width)
    for b in range(blocks):
        total = jnp.zeros((side, width), F32)
        for k in range(0, per_block, 2):
            tile = jnp.concatenate([tiles[b * per_block + k], tiles[b * per_block + k + 1]], axis=1)
            source = jnp.concatenate([extended[ids[b, k]], extended[ids[b, k + 1]]], axis=0)
            total = total + dot(tile, source)
        aggregated[pl.ds(b * side, side), :] = total.astype(BF16)

    edges = pos.shape[1]
    chunk = 512
    lane = lax.broadcasted_iota(jnp.int32, (chunk, side), 1)
    for c in range(4 * edges // chunk):
        end, offset = divmod(c * chunk, edges)
        source = (pos, neg)[end // 2]
        turned = [
            jnp.broadcast_to(
                source[pl.ds(end % 2, 1), pl.ds(offset + part * side, side)], (side, side)
            ).T
            for part in range(chunk // side)
        ]
        index = jnp.concatenate(turned, axis=0)
        onehot = jnp.concatenate(
            [(index == lane + part * side).astype(F32).astype(BF16) for part in range(rows // side)],
            axis=1,
        )
        picked[pl.ds(c * chunk, chunk), :] = dot(onehot, aggregated[...]).astype(BF16)

    half = jnp.zeros((width, width), F32)
    for sign in (0, 1):
        first = picked[pl.ds(2 * sign * edges, edges), :]
        second = picked[pl.ds((2 * sign + 1) * edges, edges), :]
        score = jnp.sum(dot(first, score_matrix[...]) * second.astype(F32), axis=1, keepdims=True)
        score = score * (1.0 / width)
        if sign == 0:
            slope = sigmoid(-score) * (-factor)
        else:
            slope = sigmoid(score) * factor
        scaled = split(slope * first.astype(F32))
        half = half + dot(scaled[0], second, ROWS) + dot(scaled[1], second, ROWS)
    full = half + half.T
    quarter = width // 2
    upper = full[:quarter, :quarter]
    lower = full[quarter:, quarter:]
    i = lax.broadcasted_iota(jnp.int32, (quarter, quarter), 0)
    j = lax.broadcasted_iota(jnp.int32, (quarter, quarter), 1)
    diagonal = jnp.sum(jnp.where(i == j, lower, 0.0), axis=0, keepdims=True)
    corner = full[:quarter, quarter:].astype(BF16)
    mixed = jnp.where(i <= j, upper, lower).astype(BF16)
    extra = jnp.broadcast_to(diagonal, (PACK_EXTRA, quarter)).astype(BF16)
    for packed in outs:
        packed[pl.ds(0, quarter), :] = corner
        packed[pl.ds(quarter, quarter), :] = mixed
        packed[pl.ds(2 * quarter, PACK_EXTRA), :] = extra


def backward_kernel(
    along,
    other,
    keep,
    gate_slope,
    proposal_slope,
    reset_slope,
    reset,
    low,
    weights_wide,
    reset_wide,
    turned_high,
    turned_low,
    adjoint_rows,
    grads,
    initial_grad,
    adjoints,
    local,
):
    steps, width = low.shape[0], low.shape[1]
    quarter = width // 2
    place, node = lax.axis_index("snap"), lax.axis_index("node")
    x, core = lax.div(place, 2), lax.rem(place, 2)
    i = lax.broadcasted_iota(jnp.int32, (quarter, quarter), 0)
    j = lax.broadcasted_iota(jnp.int32, (quarter, quarter), 1)

    for t in range(steps):
        turn = lax.rem(x - t // 2 + RING, RING)
        piece = jnp.where(core == t % 2, along[turn], other[turn])
        corner = piece[:quarter]
        mixed = piece[quarter : 2 * quarter].astype(F32)
        diagonal = piece[2 * quarter :].astype(F32)[0:1]
        turned = mixed.T
        upper = jnp.where(i <= j, mixed, turned).astype(BF16)
        lower = jnp.where(i > j, mixed, jnp.where(i < j, turned, diagonal)).astype(BF16)
        whole = jnp.concatenate(
            [
                jnp.concatenate([upper, corner], axis=1),
                jnp.concatenate([corner.T, lower], axis=1),
            ],
            axis=0,
        )
        local[t] = dot(whole, low[t])

    def gate(k, parts):
        return dot3((turned_high[k], turned_low[k]), parts)

    grads[...] = jnp.zeros_like(grads)

    def step(s, carry):
        t = steps - 1 - s
        g = local[t] + carry
        adjoints[t] = g
        d2 = g * proposal_slope[t]
        d2_parts = split(d2)
        mixed = gate(3, d2_parts)
        d0 = g * gate_slope[t]
        d0_parts = split(d0)
        fresh = g * keep[t] + (gate(0, d0_parts) + gate(2, d2_parts))
        d1 = mixed * reset_slope[t]
        d1_parts = split(d1)
        fresh = fresh + mixed * reset[t] + gate(1, d1_parts)
        lanes = pl.ds(pl.multiple_of(t * width, width), width)
        before = weights_wide[:, lanes]
        grads[0] += dot(d0_parts[0], before, LANES)
        grads[1] += dot(d1_parts[0], before, LANES)
        grads[2] += dot(d2_parts[0], before, LANES)
        grads[3] += dot(d2_parts[0], reset_wide[:, lanes], LANES)
        grads[4] += d0
        grads[5] += d1
        grads[6] += d2
        return fresh

    initial_grad[...] = lax.fori_loop(0, steps, step, jnp.zeros((width, width), F32))
    share = adjoint_rows.shape[0]
    start = pl.multiple_of(node * share, share)
    adjoint_rows[...] = adjoints[place, pl.ds(start, share), :]


def params(megabytes):
    return pltpu.CompilerParams(vmem_limit_bytes=megabytes * 2**20)


VMEM = pl.BlockSpec(memory_space=pltpu.VMEM)
SMEM = pl.BlockSpec(memory_space=pltpu.SMEM)
HBM = pl.BlockSpec(memory_space=pltpu.HBM)


def ring_parts(copies, axis, stride, count):
    size = lax.axis_size(axis)
    span = stride * count
    parts = []
    for turn in sorted(range(1, count), key=lambda k: -min(k, count - k)):
        route = [(i, i - i % span + (i % span + turn * stride) % span) for i in range(size)]
        parts.append(lax.ppermute(copies[turn], axis, route))
    return parts


def sum_kernel(own, first, second, third, *copies):
    total = (own[...].astype(F32) + first[...].astype(F32)) + (
        second[...].astype(F32) + third[...].astype(F32)
    )
    total = total.astype(BF16)
    for copy in copies:
        copy[...] = total


def ring_sum(copies, axis, stride, count):
    parts = ring_parts(copies, axis, stride, count)
    like = jax.ShapeDtypeStruct(copies[0].shape, BF16)
    return pl.pallas_call(
        sum_kernel,
        out_shape=[like] * RING,
        in_specs=[VMEM] * RING,
        out_specs=[VMEM] * RING,
        compiler_params=params(4),
        name="ring_sum",
    )(copies[0], *parts)


def body(
    features, tile_ids, tile_values, pos_edges, neg_edges, initial_weight, gate_mats, gate_bias
):
    snap_count = lax.axis_size("snap")
    node_count = lax.axis_size("node")
    own = features[0]
    rows, width = own.shape
    side = tile_values.shape[-1]
    square = (snap_count, width, width)

    even_pairs = [(i, i ^ 1) for i in range(node_count)]
    odd_pairs = [(i, (i - 1 + 2 * (i % 2)) % node_count) for i in range(node_count)]
    even_side = lax.ppermute(own, "node", even_pairs)
    odd_side = lax.ppermute(own, "node", odd_pairs)

    wide = jax.ShapeDtypeStruct(square, F32)
    thin = jax.ShapeDtypeStruct(square, BF16)
    long = jax.ShapeDtypeStruct((width, snap_count * width), BF16)
    mats = jax.ShapeDtypeStruct((4, width, width), BF16)
    *states, score_matrix = pl.pallas_call(
        forward_kernel,
        out_shape=[wide] * 5
        + [thin, long, long, mats, mats, jax.ShapeDtypeStruct((width, width), BF16)],
        in_specs=[HBM] * 3,
        out_specs=[VMEM] * 11,
        scratch_shapes=[
            pltpu.VMEM((width, width), F32),
            pltpu.VMEM((4, width, width), F32),
            pltpu.VMEM((3, width, width), F32),
            pltpu.VMEM((4, width, width), BF16),
            pltpu.VMEM((4, width, width), BF16),
            pltpu.SemaphoreType.DMA((8,)),
        ],
        compiler_params=params(16),
        name="forward_chain",
    )(
        *(
            pltpu.with_memory_space_constraint(array, pltpu.HBM)
            for array in (initial_weight, gate_mats, gate_bias)
        )
    )

    factor = float(rows * node_count) ** (-0.5)
    pack_rows = width + PACK_EXTRA
    copies = pl.pallas_call(
        functools.partial(edge_kernel, factor),
        out_shape=[jax.ShapeDtypeStruct((pack_rows, width // 2), BF16)] * RING,
        in_specs=[SMEM] + [VMEM] * 7,
        out_specs=[VMEM] * RING,
        scratch_shapes=[
            pltpu.VMEM(((rows + 2 * HALO) // side, side, width), BF16),
            pltpu.VMEM((rows, width), BF16),
            pltpu.VMEM((4 * pos_edges.shape[-1], width), BF16),
        ],
        compiler_params=params(16),
        name="edge_products",
    )(
        tile_ids[0],
        own,
        even_side,
        odd_side,
        tile_values.reshape(-1, side, side),
        pos_edges[0],
        neg_edges[0],
        score_matrix,
    )

    copies = ring_sum(copies, "node", 1, RING)
    copies = ring_sum(copies, "node", RING, node_count // RING)
    far, near, back = ring_parts(copies, "snap", 2, snap_count // 2)
    along = jnp.stack([copies[0], near, far, back])
    other = lax.ppermute(along, "snap", [(i, i ^ 1) for i in range(snap_count)])

    share = width // node_count
    adjoint_rows, grads, initial_grad = pl.pallas_call(
        backward_kernel,
        out_shape=[
            jax.ShapeDtypeStruct((share, width), F32),
            jax.ShapeDtypeStruct((7, width, width), F32),
            jax.ShapeDtypeStruct((width, width), F32),
        ],
        in_specs=[VMEM] * 12,
        out_specs=[VMEM] * 3,
        scratch_shapes=[pltpu.VMEM(square, F32)] * 2,
        compiler_params=params(16),
        name="backward_chain",
    )(along, other, *states)
    return adjoint_rows[None], grads, initial_grad


def solution(mesh):
    placed = (
        P("snap", "node", None),
        P("snap", "node", None),
        P("snap", "node", None, None, None),
        P("snap", None, "node"),
        P("snap", None, "node"),
        P(),
        P(),
        P(),
    )
    return jax.shard_map(
        body,
        mesh=mesh,
        in_specs=placed,
        out_specs=(P("snap", "node", None), P(), P()),
        check_vma=False,
    )
```

```python
import functools

import jax
import jax.numpy as jnp
from jax import lax
from jax.experimental import pallas as pl
from jax.experimental.pallas import tpu as pltpu
from jax.sharding import PartitionSpec as P

HALO = 1024
RING = 4
PACK_EXTRA = 16
F32 = jnp.float32
BF16 = jnp.bfloat16
INNER = (((1,), (0,)), ((), ()))
LANES = (((1,), (1,)), ((), ()))
ROWS = (((0,), (0,)), ((), ()))


def split(value):
    high = value.astype(BF16)
    return high, (value - high.astype(F32)).astype(BF16)


def dot(left, right, dims=INNER):
    return lax.dot_general(left, right, dims, preferred_element_type=F32)


def dot3(left, right, dims=INNER):
    return (
        dot(left[0], right[0], dims) + dot(left[0], right[1], dims) + dot(left[1], right[0], dims)
    )


def sigmoid(value):
    return 0.5 * jnp.tanh(0.5 * value) + 0.5


def load_gates(start_hbm, mats_hbm, bias_hbm, start, mats, bias, mats_high, mats_low, sems):
    copies = [pltpu.make_async_copy(start_hbm, start, sems.at[0])]
    copies += [
        pltpu.make_async_copy(mats_hbm.at[k], mats.at[k], sems.at[1 + k]) for k in range(4)
    ]
    copies += [
        pltpu.make_async_copy(bias_hbm.at[k], bias.at[k], sems.at[5 + k]) for k in range(3)
    ]
    for copy in copies:
        copy.start()
    for copy in copies[:5]:
        copy.wait()
    for k in range(4):
        mats_high[k], mats_low[k] = split(mats[k])
    for copy in copies[5:]:
        copy.wait()


def gate_step(weight, bias, mats_high, mats_low):
    def gate(k, parts):
        return dot3((mats_high[k], mats_low[k]), parts)

    parts = split(weight)
    r = sigmoid(gate(1, parts) + bias[1])
    mixed = r * weight
    mixed_parts = split(mixed)
    u_in = gate(0, parts)
    c_in = gate(2, parts)
    u = sigmoid(u_in + bias[0])
    c = jnp.tanh(c_in + gate(3, mixed_parts) + bias[2])
    return u, r, c, mixed, (1.0 - u) * weight + u * c


def write_score_matrix(low, score_matrix):
    own = low[lax.axis_index("snap")]
    score_matrix[...] = dot(own, own, LANES).astype(BF16)


def early_kernel(start_hbm, mats_hbm, bias_hbm, score_matrix, low, *scratch):
    start, mats, bias, mats_high, mats_low, sems = scratch

    @pl.when(lax.rem(lax.axis_index("snap"), 2) == 1)
    def _():
        load_gates(start_hbm, mats_hbm, bias_hbm, *scratch)
        weight = start[...]
        for t in range(low.shape[0]):
            weight = gate_step(weight, bias, mats_high, mats_low)[-1]
            low[t] = weight.astype(BF16)
        write_score_matrix(low, score_matrix)


def late_kernel(
    start_hbm,
    mats_hbm,
    bias_hbm,
    early_score_matrix,
    keep,
    gate_slope,
    proposal_slope,
    reset_slope,
    reset,
    low,
    weights_wide,
    reset_wide,
    turned_high,
    turned_low,
    score_matrix,
    *scratch,
):
    start, mats, bias, mats_high, mats_low, sems = scratch
    steps, width = low.shape[0], low.shape[1]
    odd = lax.rem(lax.axis_index("snap"), 2) == 1
    load_gates(start_hbm, mats_hbm, bias_hbm, *scratch)
    weight = start[...]
    for t in range(steps):
        u, r, c, mixed, fresh = gate_step(weight, bias, mats_high, mats_low)
        keep[t] = 1.0 - u
        reset[t] = r
        gate_slope[t] = (c - weight) * (u * (1.0 - u))
        proposal_slope[t] = u * (1.0 - c * c)
        reset_slope[t] = mixed * (1.0 - r)
        lanes = pl.ds(t * width, width)
        weights_wide[:, lanes] = weight.astype(BF16)
        reset_wide[:, lanes] = mixed.astype(BF16)
        weight = fresh
        low[t] = weight.astype(BF16)
    for k in range(4):
        turned_high[k] = mats_high[k].T
    for k in range(2):
        turned_low[k] = mats_low[k + 2].T

    @pl.when(odd)
    def _():
        score_matrix[...] = early_score_matrix[...]

    @pl.when(jnp.logical_not(odd))
    def _():
        write_score_matrix(low, score_matrix)


def edge_kernel(
    factor,
    ids,
    own,
    even_side,
    odd_side,
    tiles,
    pos,
    neg,
    score_matrix,
    *refs,
):
    *outs, extended, aggregated, picked = refs
    rows, width = own.shape
    side = tiles.shape[1]
    blocks = rows // side
    per_block = ids.shape[1]
    node, ends = lax.axis_index("node"), lax.axis_size("node") - 1
    odd = lax.rem(node, 2)
    inside = (node > 0) & (node < ends)
    far = jnp.where(inside, odd_side[...], jnp.zeros_like(odd_side))
    extended[pl.ds(2 * blocks * (1 - odd), blocks)] = even_side[...].reshape(blocks, side, width)
    extended[pl.ds(blocks, blocks)] = own[...].reshape(blocks, side, width)
    extended[pl.ds(2 * blocks * odd, blocks)] = far.reshape(blocks, side, width)
    for b in range(blocks):
        total = jnp.zeros((side, width), F32)
        for k in range(0, per_block, 2):
            tile = jnp.concatenate([tiles[b * per_block + k], tiles[b * per_block + k + 1]], axis=1)
            source = jnp.concatenate([extended[ids[b, k]], extended[ids[b, k + 1]]], axis=0)
            total = total + dot(tile, source)
        aggregated[pl.ds(b * side, side), :] = total.astype(BF16)

    edges = pos.shape[1]
    chunk = 512
    lane = lax.broadcasted_iota(jnp.int32, (chunk, side), 1)
    for c in range(4 * edges // chunk):
        end, offset = divmod(c * chunk, edges)
        source = (pos, neg)[end // 2]
        turned = [
            jnp.broadcast_to(
                source[pl.ds(end % 2, 1), pl.ds(offset + part * side, side)], (side, side)
            ).T
            for part in range(chunk // side)
        ]
        index = jnp.concatenate(turned, axis=0)
        onehot = jnp.concatenate(
            [(index == lane + part * side).astype(F32).astype(BF16) for part in range(rows // side)],
            axis=1,
        )
        picked[pl.ds(c * chunk, chunk), :] = dot(onehot, aggregated[...]).astype(BF16)

    half = jnp.zeros((width, width), F32)
    for sign in (0, 1):
        first = picked[pl.ds(2 * sign * edges, edges), :]
        second = picked[pl.ds((2 * sign + 1) * edges, edges), :]
        score = jnp.sum(dot(first, score_matrix[...]) * second.astype(F32), axis=1, keepdims=True)
        score = score * (1.0 / width)
        if sign == 0:
            slope = sigmoid(-score) * (-factor)
        else:
            slope = sigmoid(score) * factor
        scaled = split(slope * first.astype(F32))
        half = half + dot(scaled[0], second, ROWS) + dot(scaled[1], second, ROWS)
    full = half + half.T
    quarter = width // 2
    upper = full[:quarter, :quarter]
    lower = full[quarter:, quarter:]
    i = lax.broadcasted_iota(jnp.int32, (quarter, quarter), 0)
    j = lax.broadcasted_iota(jnp.int32, (quarter, quarter), 1)
    diagonal = jnp.sum(jnp.where(i == j, lower, 0.0), axis=0, keepdims=True)
    corner = full[:quarter, quarter:].astype(BF16)
    mixed = jnp.where(i <= j, upper, lower).astype(BF16)
    extra = jnp.broadcast_to(diagonal, (PACK_EXTRA, quarter)).astype(BF16)
    for packed in outs:
        packed[pl.ds(0, quarter), :] = corner
        packed[pl.ds(quarter, quarter), :] = mixed
        packed[pl.ds(2 * quarter, PACK_EXTRA), :] = extra


def local_gradient(pieces, low, core, s, out):
    width = low.shape[1]
    quarter = width // 2
    i = lax.broadcasted_iota(jnp.int32, (quarter, quarter), 0)
    j = lax.broadcasted_iota(jnp.int32, (quarter, quarter), 1)
    x = lax.div(lax.axis_index("snap"), 2)
    piece = pieces[lax.rem(x - s + RING, RING)]
    corner = piece[:quarter]
    mixed = piece[quarter : 2 * quarter].astype(F32)
    diagonal = piece[2 * quarter :].astype(F32)[0:1]
    turned = mixed.T
    upper = jnp.where(i <= j, mixed, turned).astype(BF16)
    lower = jnp.where(i > j, mixed, jnp.where(i < j, turned, diagonal)).astype(BF16)
    whole = jnp.concatenate(
        [
            jnp.concatenate([upper, corner], axis=1),
            jnp.concatenate([corner.T, lower], axis=1),
        ],
        axis=0,
    )
    out[s] = dot(whole, low[2 * s + core])


def local_kernel(along, low, mine):
    core = lax.rem(lax.axis_index("snap"), 2)
    for s in range(mine.shape[0]):
        local_gradient(along, low, core, s, mine)


def backward_kernel(
    mine,
    other,
    keep,
    gate_slope,
    proposal_slope,
    reset_slope,
    reset,
    low,
    weights_wide,
    reset_wide,
    turned_high,
    turned_low,
    adjoint_rows,
    grads,
    initial_grad,
    adjoints,
    others,
):
    steps, width = low.shape[0], low.shape[1]
    place, node = lax.axis_index("snap"), lax.axis_index("node")
    core = lax.rem(place, 2)
    for s in range(steps // 2):
        local_gradient(other, low, 1 - core, s, others)

    def gate(k, parts):
        return dot3((turned_high[k], turned_low[k - 2]), parts)

    def gate_once(k, part):
        return dot(turned_high[k], part)

    grads[...] = jnp.zeros_like(grads)

    def step(s, carry):
        t = steps - 1 - s
        g = jnp.where(lax.rem(t, 2) == core, mine[lax.div(t, 2)], others[lax.div(t, 2)]) + carry
        adjoints[t] = g
        d2 = g * proposal_slope[t]
        d2_parts = split(d2)
        mixed = gate(3, d2_parts)
        d0 = g * gate_slope[t]
        d0_high = d0.astype(BF16)
        fresh = g * keep[t] + (gate_once(0, d0_high) + gate(2, d2_parts))
        d1 = mixed * reset_slope[t]
        d1_high = d1.astype(BF16)
        fresh = fresh + mixed * reset[t] + gate_once(1, d1_high)
        lanes = pl.ds(pl.multiple_of(t * width, width), width)
        before = weights_wide[:, lanes]
        grads[0] += dot(d0_high, before, LANES)
        grads[1] += dot(d1_high, before, LANES)
        grads[2] += dot(d2_parts[0], before, LANES)
        grads[3] += dot(d2_parts[0], reset_wide[:, lanes], LANES)
        grads[4] += d0
        grads[5] += d1
        grads[6] += d2
        return fresh

    initial_grad[...] = lax.fori_loop(0, steps, step, jnp.zeros((width, width), F32))
    share = adjoint_rows.shape[0]
    start = pl.multiple_of(node * share, share)
    adjoint_rows[...] = adjoints[place, pl.ds(start, share), :]


def params(megabytes):
    return pltpu.CompilerParams(vmem_limit_bytes=megabytes * 2**20)


VMEM = pl.BlockSpec(memory_space=pltpu.VMEM)
SMEM = pl.BlockSpec(memory_space=pltpu.SMEM)
HBM = pl.BlockSpec(memory_space=pltpu.HBM)


def ring_parts(copies, axis, stride, count):
    size = lax.axis_size(axis)
    span = stride * count
    parts = []
    for turn in sorted(range(1, count), key=lambda k: -min(k, count - k)):
        route = [(i, i - i % span + (i % span + turn * stride) % span) for i in range(size)]
        parts.append(lax.ppermute(copies[turn], axis, route))
    return parts


def sum_kernel(own, first, second, third, *copies):
    total = (own[...].astype(F32) + first[...].astype(F32)) + (
        second[...].astype(F32) + third[...].astype(F32)
    )
    total = total.astype(BF16)
    for copy in copies:
        copy[...] = total


def ring_sum(copies, axis, stride, count):
    parts = ring_parts(copies, axis, stride, count)
    like = jax.ShapeDtypeStruct(copies[0].shape, BF16)
    return pl.pallas_call(
        sum_kernel,
        out_shape=[like] * RING,
        in_specs=[VMEM] * RING,
        out_specs=[VMEM] * RING,
        compiler_params=params(4),
        name="ring_sum",
    )(copies[0], *parts)


def body(
    features, tile_ids, tile_values, pos_edges, neg_edges, initial_weight, gate_mats, gate_bias
):
    snap_count = lax.axis_size("snap")
    node_count = lax.axis_size("node")
    own = features[0]
    rows, width = own.shape
    side = tile_values.shape[-1]
    square = (snap_count, width, width)

    sources = [
        pltpu.with_memory_space_constraint(array, pltpu.HBM)
        for array in (initial_weight, gate_mats, gate_bias)
    ]
    gate_scratch = [
        pltpu.VMEM((width, width), F32),
        pltpu.VMEM((4, width, width), F32),
        pltpu.VMEM((3, width, width), F32),
        pltpu.VMEM((4, width, width), BF16),
        pltpu.VMEM((4, width, width), BF16),
        pltpu.SemaphoreType.DMA((8,)),
    ]
    flat = jax.ShapeDtypeStruct((width, width), BF16)
    early_score_matrix = pl.pallas_call(
        early_kernel,
        out_shape=flat,
        in_specs=[HBM] * 3,
        out_specs=VMEM,
        scratch_shapes=[pltpu.VMEM(square, BF16)] + gate_scratch,
        compiler_params=params(10),
        name="forward_early",
    )(*sources)
    own, early_score_matrix = lax.optimization_barrier((own, early_score_matrix))
    even_pairs = [(i, i ^ 1) for i in range(node_count)]
    odd_pairs = [(i, (i - 1 + 2 * (i % 2)) % node_count) for i in range(node_count)]
    even_side = lax.ppermute(own, "node", even_pairs)
    odd_side = lax.ppermute(own, "node", odd_pairs)

    wide = jax.ShapeDtypeStruct(square, F32)
    long = jax.ShapeDtypeStruct((width, snap_count * width), BF16)
    outs = [wide] * 5 + [jax.ShapeDtypeStruct(square, BF16), long, long]
    outs += [jax.ShapeDtypeStruct((k, width, width), BF16) for k in (4, 2)] + [flat]
    *states, score_matrix = pl.pallas_call(
        late_kernel,
        out_shape=outs,
        in_specs=[HBM] * 3 + [VMEM],
        out_specs=[VMEM] * len(outs),
        scratch_shapes=gate_scratch,
        compiler_params=params(10),
        name="forward_late",
    )(*sources, early_score_matrix)

    factor = float(rows * node_count) ** (-0.5)
    pack_rows = width + PACK_EXTRA
    copies = pl.pallas_call(
        functools.partial(edge_kernel, factor),
        out_shape=[jax.ShapeDtypeStruct((pack_rows, width // 2), BF16)] * RING,
        in_specs=[SMEM] + [VMEM] * 7,
        out_specs=[VMEM] * RING,
        scratch_shapes=[
            pltpu.VMEM(((rows + 2 * HALO) // side, side, width), BF16),
            pltpu.VMEM((rows, width), BF16),
            pltpu.VMEM((4 * pos_edges.shape[-1], width), BF16),
        ],
        compiler_params=params(16),
        name="edge_products",
    )(
        tile_ids[0],
        own,
        even_side,
        odd_side,
        tile_values.reshape(-1, side, side),
        pos_edges[0],
        neg_edges[0],
        score_matrix,
    )

    copies = ring_sum(copies, "node", 1, RING)
    copies = ring_sum(copies, "node", RING, node_count // RING)
    far, near, back = ring_parts(copies, "snap", 2, snap_count // 2)
    along = jnp.stack([copies[0], near, far, back])
    other = lax.ppermute(along, "snap", [(i, i ^ 1) for i in range(snap_count)])

    half = (snap_count // 2, width, width)
    mine = pl.pallas_call(
        local_kernel,
        out_shape=jax.ShapeDtypeStruct(half, F32),
        in_specs=[VMEM] * 2,
        out_specs=VMEM,
        compiler_params=params(8),
        name="local_gradients",
    )(along, states[5])

    share = width // node_count
    adjoint_rows, grads, initial_grad = pl.pallas_call(
        backward_kernel,
        out_shape=[
            jax.ShapeDtypeStruct((share, width), F32),
            jax.ShapeDtypeStruct((7, width, width), F32),
            jax.ShapeDtypeStruct((width, width), F32),
        ],
        in_specs=[VMEM] * 12,
        out_specs=[VMEM] * 3,
        scratch_shapes=[pltpu.VMEM(square, F32), pltpu.VMEM(half, F32)],
        compiler_params=params(16),
        name="backward_chain",
    )(mine, other, *states)
    return adjoint_rows[None], grads, initial_grad


def solution(mesh):
    placed = (
        P("snap", "node", None),
        P("snap", "node", None),
        P("snap", "node", None, None, None),
        P("snap", None, "node"),
        P("snap", None, "node"),
        P(),
        P(),
        P(),
    )
    return jax.shard_map(
        body,
        mesh=mesh,
        in_specs=placed,
        out_specs=(P("snap", "node", None), P(), P()),
        check_vma=False,
    )
```

```python
import functools

import jax
import jax.numpy as jnp
from jax import lax
from jax.experimental import pallas as pl
from jax.experimental.pallas import tpu as pltpu
from jax.sharding import PartitionSpec as P

HALO = 1024
RING = 4
STRIDE = 3
PACK_EXTRA = 16
F32 = jnp.float32
BF16 = jnp.bfloat16
INNER = (((1,), (0,)), ((), ()))
LANES = (((1,), (1,)), ((), ()))
ROWS = (((0,), (0,)), ((), ()))


def split(value):
    high = value.astype(BF16)
    return high, (value - high.astype(F32)).astype(BF16)


def dot(left, right, dims=INNER):
    return lax.dot_general(left, right, dims, preferred_element_type=F32)


def dot3(left, right, dims=INNER):
    return (
        dot(left[0], right[0], dims) + dot(left[0], right[1], dims) + dot(left[1], right[0], dims)
    )


def sigmoid(value):
    return 0.5 * jnp.tanh(0.5 * value) + 0.5


def load_gates(start_hbm, mats_hbm, bias_hbm, start, mats, bias, mats_high, mats_low, sems):
    copies = [pltpu.make_async_copy(start_hbm, start, sems.at[0])]
    copies += [
        pltpu.make_async_copy(mats_hbm.at[k], mats.at[k], sems.at[1 + k]) for k in range(4)
    ]
    copies += [
        pltpu.make_async_copy(bias_hbm.at[k], bias.at[k], sems.at[5 + k]) for k in range(3)
    ]
    for copy in copies:
        copy.start()
    for copy in copies[:5]:
        copy.wait()
    for k in range(4):
        mats_high[k], mats_low[k] = split(mats[k])
    for copy in copies[5:]:
        copy.wait()


def gate_step(weight, bias, mats_high, mats_low):
    def gate(k, parts):
        return dot3((mats_high[k], mats_low[k]), parts)

    parts = split(weight)
    r = sigmoid(dot(mats_high[1], parts[0]) + bias[1])
    mixed = r * weight
    mixed_parts = split(mixed)
    c_in = gate(2, parts)
    c_in = c_in + gate(3, mixed_parts)
    u_in = gate(0, parts)
    u = sigmoid(u_in + bias[0])
    c = jnp.tanh(c_in + bias[2])
    return u, r, c, mixed, (1.0 - u) * weight + u * c


def write_score_matrix(low, score_matrix):
    own = low[lax.axis_index("snap")]
    score_matrix[...] = dot(own, own, LANES).astype(BF16)


def early_kernel(start_hbm, mats_hbm, bias_hbm, before, score_matrix, low, *scratch):
    start, mats, bias, mats_high, mats_low, sems = scratch

    @pl.when(lax.rem(lax.axis_index("snap"), 2) == 1)
    def _():
        load_gates(start_hbm, mats_hbm, bias_hbm, *scratch)
        weight = start[...]
        for t in range(low.shape[0]):
            if t > 0 and t % STRIDE == 0:
                before[t // STRIDE - 1] = weight
            weight = gate_step(weight, bias, mats_high, mats_low)[-1]
            low[t] = weight.astype(BF16)
        write_score_matrix(low, score_matrix)


def late_kernel(
    start_hbm,
    mats_hbm,
    bias_hbm,
    before,
    early_score_matrix,
    keep,
    gate_slope,
    proposal_slope,
    reset_slope,
    reset,
    low,
    weights_wide,
    reset_wide,
    turned_high,
    turned_low,
    score_matrix,
    *scratch,
):
    start, mats, bias, mats_high, mats_low, sems = scratch
    steps, width = low.shape[0], low.shape[1]
    odd = lax.rem(lax.axis_index("snap"), 2) == 1
    load_gates(start_hbm, mats_hbm, bias_hbm, *scratch)

    def record(t, weight):
        u, r, c, mixed, fresh = gate_step(weight, bias, mats_high, mats_low)
        keep[t] = 1.0 - u
        reset[t] = r
        gate_slope[t] = (c - weight) * (u * (1.0 - u))
        proposal_slope[t] = u * (1.0 - c * c)
        reset_slope[t] = mixed * (1.0 - r)
        lanes = pl.ds(t * width, width)
        weights_wide[:, lanes] = weight.astype(BF16)
        reset_wide[:, lanes] = mixed.astype(BF16)
        low[t] = fresh.astype(BF16)
        return fresh

    @pl.when(odd)
    def _():
        weights = [start[...]] + [before[k] for k in range(before.shape[0])]
        for s in range(STRIDE):
            for k in range(len(weights)):
                if k * STRIDE + s < steps:
                    weights[k] = record(k * STRIDE + s, weights[k])
        score_matrix[...] = early_score_matrix[...]

    @pl.when(jnp.logical_not(odd))
    def _():
        weight = start[...]
        for t in range(steps):
            weight = record(t, weight)
        write_score_matrix(low, score_matrix)

    for k in range(4):
        turned_high[k] = mats_high[k].T
    for k in range(2):
        turned_low[k] = mats_low[k + 2].T


def edge_kernel(
    factor,
    ids,
    own,
    even_side,
    odd_side,
    tiles,
    pos,
    neg,
    score_matrix,
    *refs,
):
    *outs, extended, aggregated, picked = refs
    rows, width = own.shape
    side = tiles.shape[1]
    blocks = rows // side
    per_block = ids.shape[1]
    picks = ids[...]
    node, ends = lax.axis_index("node"), lax.axis_size("node") - 1
    odd = lax.rem(node, 2)
    inside = (node > 0) & (node < ends)
    far = jnp.where(inside, odd_side[...], jnp.zeros_like(odd_side))
    extended[pl.ds(2 * blocks * (1 - odd), blocks)] = even_side[...].reshape(blocks, side, width)
    extended[pl.ds(blocks, blocks)] = own[...].reshape(blocks, side, width)
    extended[pl.ds(2 * blocks * odd, blocks)] = far.reshape(blocks, side, width)
    for b in range(blocks):
        total = jnp.zeros((side, width), F32)
        for k in range(0, per_block, 2):
            tile = jnp.concatenate([tiles[b * per_block + k], tiles[b * per_block + k + 1]], axis=1)
            source = jnp.concatenate([extended[picks[b, k]], extended[picks[b, k + 1]]], axis=0)
            total = total + dot(tile, source)
        aggregated[pl.ds(b * side, side), :] = total.astype(BF16)

    edges = pos.shape[1]
    chunk = 512
    lane = lax.broadcasted_iota(jnp.int32, (chunk, side), 1)
    for c in range(4 * edges // chunk):
        end, offset = divmod(c * chunk, edges)
        source = (pos, neg)[end // 2]
        turned = [
            jnp.broadcast_to(
                source[pl.ds(end % 2, 1), pl.ds(offset + part * side, side)], (side, side)
            ).T
            for part in range(chunk // side)
        ]
        index = jnp.concatenate(turned, axis=0)
        onehot = jnp.concatenate(
            [(index == lane + part * side).astype(F32).astype(BF16) for part in range(rows // side)],
            axis=1,
        )
        picked[pl.ds(c * chunk, chunk), :] = dot(onehot, aggregated[...]).astype(BF16)

    half = jnp.zeros((width, width), F32)
    for sign in (0, 1):
        first = picked[pl.ds(2 * sign * edges, edges), :]
        second = picked[pl.ds((2 * sign + 1) * edges, edges), :]
        score = jnp.sum(dot(first, score_matrix[...]) * second.astype(F32), axis=1, keepdims=True)
        score = score * (1.0 / width)
        if sign == 0:
            slope = sigmoid(-score) * (-factor)
        else:
            slope = sigmoid(score) * factor
        scaled = (slope * first.astype(F32)).astype(BF16)
        half = half + dot(scaled, second, ROWS)
    full = half + half.T
    quarter = width // 2
    upper = full[:quarter, :quarter]
    lower = full[quarter:, quarter:]
    i = lax.broadcasted_iota(jnp.int32, (quarter, quarter), 0)
    j = lax.broadcasted_iota(jnp.int32, (quarter, quarter), 1)
    diagonal = jnp.sum(jnp.where(i == j, lower, 0.0), axis=0, keepdims=True)
    corner = full[:quarter, quarter:].astype(BF16)
    mixed = jnp.where(i <= j, upper, lower).astype(BF16)
    extra = jnp.broadcast_to(diagonal, (PACK_EXTRA, quarter)).astype(BF16)
    for packed in outs:
        packed[pl.ds(0, quarter), :] = corner
        packed[pl.ds(quarter, quarter), :] = mixed
        packed[pl.ds(2 * quarter, PACK_EXTRA), :] = extra


def local_gradient(pieces, low, core, s, out):
    width = low.shape[1]
    quarter = width // 2
    i = lax.broadcasted_iota(jnp.int32, (quarter, quarter), 0)
    j = lax.broadcasted_iota(jnp.int32, (quarter, quarter), 1)
    x = lax.div(lax.axis_index("snap"), 2)
    piece = pieces[lax.rem(x - s + RING, RING)]
    corner = piece[:quarter]
    mixed = piece[quarter : 2 * quarter].astype(F32)
    diagonal = piece[2 * quarter :].astype(F32)[0:1]
    turned = mixed.T
    upper = jnp.where(i <= j, mixed, turned).astype(BF16)
    lower = jnp.where(i > j, mixed, jnp.where(i < j, turned, diagonal)).astype(BF16)
    whole = jnp.concatenate(
        [
            jnp.concatenate([upper, corner], axis=1),
            jnp.concatenate([corner.T, lower], axis=1),
        ],
        axis=0,
    )
    out[s] = dot(whole, low[2 * s + core])


def local_kernel(along, low, mine):
    core = lax.rem(lax.axis_index("snap"), 2)
    for s in range(mine.shape[0]):
        local_gradient(along, low, core, s, mine)


def backward_kernel(
    mine,
    other,
    keep,
    gate_slope,
    proposal_slope,
    reset_slope,
    reset,
    low,
    weights_wide,
    reset_wide,
    turned_high,
    turned_low,
    adjoint_rows,
    grads,
    initial_grad,
    adjoints,
    others,
):
    steps, width = low.shape[0], low.shape[1]
    place, node = lax.axis_index("snap"), lax.axis_index("node")
    core = lax.rem(place, 2)
    for s in range(steps // 2):
        local_gradient(other, low, 1 - core, s, others)

    def gate(k, parts):
        return dot3((turned_high[k], turned_low[k - 2]), parts)

    def gate_once(k, part):
        return dot(turned_high[k], part)

    grads[...] = jnp.zeros_like(grads)

    def step(s, carry):
        t = steps - 1 - s
        g = jnp.where(lax.rem(t, 2) == core, mine[lax.div(t, 2)], others[lax.div(t, 2)]) + carry
        adjoints[t] = g
        d2 = g * proposal_slope[t]
        d2_parts = split(d2)
        mixed = gate(3, d2_parts)
        d0 = g * gate_slope[t]
        d0_high = d0.astype(BF16)
        fresh = g * keep[t] + (gate_once(0, d0_high) + gate(2, d2_parts))
        d1 = mixed * reset_slope[t]
        d1_high = d1.astype(BF16)
        fresh = fresh + mixed * reset[t] + gate_once(1, d1_high)
        lanes = pl.ds(pl.multiple_of(t * width, width), width)
        before = weights_wide[:, lanes]
        grads[0] += dot(d0_high, before, LANES)
        grads[1] += dot(d1_high, before, LANES)
        grads[2] += dot(d2_parts[0], before, LANES)
        grads[3] += dot(d2_parts[0], reset_wide[:, lanes], LANES)
        grads[4] += d0
        grads[5] += d1
        grads[6] += d2
        return fresh

    initial_grad[...] = lax.fori_loop(0, steps, step, jnp.zeros((width, width), F32))
    share = adjoint_rows.shape[0]
    start = pl.multiple_of(node * share, share)
    adjoint_rows[...] = adjoints[place, pl.ds(start, share), :]


def params(megabytes):
    return pltpu.CompilerParams(vmem_limit_bytes=megabytes * 2**20)


VMEM = pl.BlockSpec(memory_space=pltpu.VMEM)
HBM = pl.BlockSpec(memory_space=pltpu.HBM)


def ring_parts(copies, axis, stride, count):
    size = lax.axis_size(axis)
    span = stride * count
    parts = []
    for turn in sorted(range(1, count), key=lambda k: -min(k, count - k)):
        route = [(i, i - i % span + (i % span + turn * stride) % span) for i in range(size)]
        parts.append(lax.ppermute(copies[turn], axis, route))
    return parts


def sum_kernel(own, first, second, third, *copies):
    total = (own[...].astype(F32) + first[...].astype(F32)) + (
        second[...].astype(F32) + third[...].astype(F32)
    )
    total = total.astype(BF16)
    for copy in copies:
        copy[...] = total


def ring_sum(copies, axis, stride, count):
    parts = ring_parts(copies, axis, stride, count)
    like = jax.ShapeDtypeStruct(copies[0].shape, BF16)
    return pl.pallas_call(
        sum_kernel,
        out_shape=[like] * RING,
        in_specs=[VMEM] * RING,
        out_specs=[VMEM] * RING,
        compiler_params=params(4),
        name="ring_sum",
    )(copies[0], *parts)


def body(
    features, tile_ids, tile_values, pos_edges, neg_edges, initial_weight, gate_mats, gate_bias
):
    snap_count = lax.axis_size("snap")
    node_count = lax.axis_size("node")
    own = features[0]
    rows, width = own.shape
    side = tile_values.shape[-1]
    square = (snap_count, width, width)

    sources = [
        pltpu.with_memory_space_constraint(array, pltpu.HBM)
        for array in (initial_weight, gate_mats, gate_bias)
    ]
    gate_scratch = [
        pltpu.VMEM((width, width), F32),
        pltpu.VMEM((4, width, width), F32),
        pltpu.VMEM((3, width, width), F32),
        pltpu.VMEM((4, width, width), BF16),
        pltpu.VMEM((4, width, width), BF16),
        pltpu.SemaphoreType.DMA((8,)),
    ]
    wide = jax.ShapeDtypeStruct(square, F32)
    flat = jax.ShapeDtypeStruct((width, width), BF16)
    before, early_score_matrix = pl.pallas_call(
        early_kernel,
        out_shape=[jax.ShapeDtypeStruct(((snap_count - 1) // STRIDE, width, width), F32), flat],
        in_specs=[HBM] * 3,
        out_specs=[VMEM] * 2,
        scratch_shapes=[pltpu.VMEM(square, BF16)] + gate_scratch,
        compiler_params=params(7),
        name="forward_early",
    )(*sources)
    own, before = lax.optimization_barrier((own, before))
    even_pairs = [(i, i ^ 1) for i in range(node_count)]
    odd_pairs = [(i, (i - 1 + 2 * (i % 2)) % node_count) for i in range(node_count)]
    even_side = lax.ppermute(own, "node", even_pairs)
    odd_side = lax.ppermute(own, "node", odd_pairs)

    long = jax.ShapeDtypeStruct((width, snap_count * width), BF16)
    outs = [wide] * 5 + [jax.ShapeDtypeStruct(square, BF16), long, long]
    outs += [jax.ShapeDtypeStruct((k, width, width), BF16) for k in (4, 2)] + [flat]
    *states, score_matrix = pl.pallas_call(
        late_kernel,
        out_shape=outs,
        in_specs=[HBM] * 3 + [VMEM] * 2,
        out_specs=[VMEM] * len(outs),
        scratch_shapes=gate_scratch,
        compiler_params=params(7),
        name="forward_late",
    )(*sources, before, early_score_matrix)

    factor = float(rows * node_count) ** (-0.5)
    pack_rows = width + PACK_EXTRA
    copies = pl.pallas_call(
        functools.partial(edge_kernel, factor),
        out_shape=[jax.ShapeDtypeStruct((pack_rows, width // 2), BF16)] * RING,
        in_specs=[VMEM] * 8,
        out_specs=[VMEM] * RING,
        scratch_shapes=[
            pltpu.VMEM(((rows + 2 * HALO) // side, side, width), BF16),
            pltpu.VMEM((rows, width), BF16),
            pltpu.VMEM((4 * pos_edges.shape[-1], width), BF16),
        ],
        compiler_params=params(9),
        name="edge_products",
    )(
        tile_ids[0],
        own,
        even_side,
        odd_side,
        tile_values.reshape(-1, side, side),
        pos_edges[0],
        neg_edges[0],
        score_matrix,
    )

    copies = ring_sum(copies, "node", 1, RING)
    copies = ring_sum(copies, "node", RING, node_count // RING)
    far, near, back = ring_parts(copies, "snap", 2, snap_count // 2)
    along = jnp.stack([copies[0], near, far, back])
    other = lax.ppermute(along, "snap", [(i, i ^ 1) for i in range(snap_count)])

    half = (snap_count // 2, width, width)
    mine = pl.pallas_call(
        local_kernel,
        out_shape=jax.ShapeDtypeStruct(half, F32),
        in_specs=[VMEM] * 2,
        out_specs=VMEM,
        compiler_params=params(8),
        name="local_gradients",
    )(along, states[5])

    share = width // node_count
    adjoint_rows, grads, initial_grad = pl.pallas_call(
        backward_kernel,
        out_shape=[
            jax.ShapeDtypeStruct((share, width), F32),
            jax.ShapeDtypeStruct((7, width, width), F32),
            jax.ShapeDtypeStruct((width, width), F32),
        ],
        in_specs=[VMEM] * 12,
        out_specs=[VMEM] * 3,
        scratch_shapes=[pltpu.VMEM(square, F32), pltpu.VMEM(half, F32)],
        compiler_params=params(9),
        name="backward_chain",
    )(mine, other, *states)
    return adjoint_rows[None], grads, initial_grad


def solution(mesh):
    placed = (
        P("snap", "node", None),
        P("snap", "node", None),
        P("snap", "node", None, None, None),
        P("snap", None, "node"),
        P("snap", None, "node"),
        P(),
        P(),
        P(),
    )
    return jax.shard_map(
        body,
        mesh=mesh,
        in_specs=placed,
        out_specs=(P("snap", "node", None), P(), P()),
        check_vma=False,
    )
```

```python
import functools

import jax
import jax.numpy as jnp
from jax import lax
from jax.experimental import pallas as pl
from jax.experimental.pallas import tpu as pltpu
from jax.sharding import PartitionSpec as P

HALO = 1024
RING = 4
STRIDE = 3
CHIPS_AT_ONCE = 2
PACK_EXTRA = 16
F32 = jnp.float32
BF16 = jnp.bfloat16
INNER = (((1,), (0,)), ((), ()))
LANES = (((1,), (1,)), ((), ()))
ROWS = (((0,), (0,)), ((), ()))


def split(value):
    high = value.astype(BF16)
    return high, (value - high.astype(F32)).astype(BF16)


def dot(left, right, dims=INNER):
    return lax.dot_general(left, right, dims, preferred_element_type=F32)


def dot3(left, right, dims=INNER):
    return (
        dot(left[0], right[0], dims) + dot(left[0], right[1], dims) + dot(left[1], right[0], dims)
    )


def sigmoid(value):
    return 0.5 * jnp.tanh(0.5 * value) + 0.5


def load_gates(start_hbm, mats_hbm, bias_hbm, start, mats, bias, mats_high, mats_low, sems):
    copies = [pltpu.make_async_copy(start_hbm, start, sems.at[0])]
    copies += [
        pltpu.make_async_copy(mats_hbm.at[k], mats.at[k], sems.at[1 + k]) for k in range(4)
    ]
    copies += [
        pltpu.make_async_copy(bias_hbm.at[k], bias.at[k], sems.at[5 + k]) for k in range(3)
    ]
    for copy in copies:
        copy.start()
    for copy in copies[:5]:
        copy.wait()
    for k in range(4):
        mats_high[k], mats_low[k] = split(mats[k])
    for copy in copies[5:]:
        copy.wait()


def gate_step(weight, bias, mats_high, mats_low):
    def gate(k, parts):
        return dot3((mats_high[k], mats_low[k]), parts)

    parts = split(weight)
    r = sigmoid(dot(mats_high[1], parts[0]) + bias[1])
    mixed = r * weight
    mixed_parts = split(mixed)
    c_in = gate(2, parts)
    c_in = c_in + gate(3, mixed_parts)
    u_in = gate(0, parts)
    u = sigmoid(u_in + bias[0])
    c = jnp.tanh(c_in + bias[2])
    return u, r, c, mixed, (1.0 - u) * weight + u * c


def write_score_matrix(low, score_matrix):
    own = low[lax.axis_index("snap")]
    score_matrix[...] = dot(own, own, LANES).astype(BF16)


def early_kernel(start_hbm, mats_hbm, bias_hbm, before, score_matrix, low, *scratch):
    start, mats, bias, mats_high, mats_low, sems = scratch

    @pl.when(lax.rem(lax.axis_index("snap"), 2) == 1)
    def _():
        load_gates(start_hbm, mats_hbm, bias_hbm, *scratch)
        weight = start[...]
        for t in range(low.shape[0]):
            if t > 0 and t % STRIDE == 0:
                before[t // STRIDE - 1] = weight
            weight = gate_step(weight, bias, mats_high, mats_low)[-1]
            low[t] = weight.astype(BF16)
        write_score_matrix(low, score_matrix)


def late_kernel(
    start_hbm,
    mats_hbm,
    bias_hbm,
    before,
    early_score_matrix,
    keep,
    gate_slope,
    proposal_slope,
    reset_slope,
    reset,
    low,
    weights_wide,
    reset_wide,
    turned_high,
    turned_low,
    score_matrix,
    *scratch,
):
    start, mats, bias, mats_high, mats_low, sems = scratch
    steps, width = low.shape[0], low.shape[1]
    odd = lax.rem(lax.axis_index("snap"), 2) == 1
    load_gates(start_hbm, mats_hbm, bias_hbm, *scratch)

    def record(t, weight):
        u, r, c, mixed, fresh = gate_step(weight, bias, mats_high, mats_low)
        keep[t] = 1.0 - u
        reset[t] = r
        gate_slope[t] = (c - weight) * (u * (1.0 - u))
        proposal_slope[t] = u * (1.0 - c * c)
        reset_slope[t] = mixed * (1.0 - r)
        lanes = pl.ds(t * width, width)
        weights_wide[:, lanes] = weight.astype(BF16)
        reset_wide[:, lanes] = mixed.astype(BF16)
        low[t] = fresh.astype(BF16)
        return fresh

    @pl.when(odd)
    def _():
        weights = [start[...]] + [before[k] for k in range(before.shape[0])]
        for s in range(STRIDE):
            for k in range(len(weights)):
                if k * STRIDE + s < steps:
                    weights[k] = record(k * STRIDE + s, weights[k])
        score_matrix[...] = early_score_matrix[...]

    @pl.when(jnp.logical_not(odd))
    def _():
        weight = start[...]
        for t in range(steps):
            weight = record(t, weight)
        write_score_matrix(low, score_matrix)

    for k in range(4):
        turned_high[k] = mats_high[k].T
    for k in range(2):
        turned_low[k] = mats_low[k + 2].T


def edge_kernel(
    factor,
    ids,
    own,
    even_side,
    odd_side,
    tiles,
    pos,
    neg,
    score_matrix,
    *refs,
):
    *outs, extended, aggregated, picked = refs
    rows, width = own.shape
    side = tiles.shape[1]
    blocks = rows // side
    per_block = ids.shape[1]
    picks = ids[...]
    node, ends = lax.axis_index("node"), lax.axis_size("node") - 1
    odd = lax.rem(node, 2)
    inside = (node > 0) & (node < ends)
    far = jnp.where(inside, odd_side[...], jnp.zeros_like(odd_side))
    extended[pl.ds(2 * blocks * (1 - odd), blocks)] = even_side[...].reshape(blocks, side, width)
    extended[pl.ds(blocks, blocks)] = own[...].reshape(blocks, side, width)
    extended[pl.ds(2 * blocks * odd, blocks)] = far.reshape(blocks, side, width)
    for b in range(blocks):
        total = jnp.zeros((side, width), F32)
        for k in range(0, per_block, 2):
            tile = jnp.concatenate([tiles[b * per_block + k], tiles[b * per_block + k + 1]], axis=1)
            source = jnp.concatenate([extended[picks[b, k]], extended[picks[b, k + 1]]], axis=0)
            total = total + dot(tile, source)
        aggregated[pl.ds(b * side, side), :] = total.astype(BF16)

    edges = pos.shape[1]
    chunk = 512
    lane = lax.broadcasted_iota(jnp.int32, (chunk, side), 1)
    for c in range(4 * edges // chunk):
        end, offset = divmod(c * chunk, edges)
        source = (pos, neg)[end // 2]
        turned = [
            jnp.broadcast_to(
                source[pl.ds(end % 2, 1), pl.ds(offset + part * side, side)], (side, side)
            ).T
            for part in range(chunk // side)
        ]
        index = jnp.concatenate(turned, axis=0)
        onehot = jnp.concatenate(
            [(index == lane + part * side).astype(F32).astype(BF16) for part in range(rows // side)],
            axis=1,
        )
        picked[pl.ds(c * chunk, chunk), :] = dot(onehot, aggregated[...]).astype(BF16)

    half = jnp.zeros((width, width), F32)
    for sign in (0, 1):
        first = picked[pl.ds(2 * sign * edges, edges), :]
        second = picked[pl.ds((2 * sign + 1) * edges, edges), :]
        score = jnp.sum(dot(first, score_matrix[...]) * second.astype(F32), axis=1, keepdims=True)
        score = score * (1.0 / width)
        if sign == 0:
            slope = sigmoid(-score) * (-factor)
        else:
            slope = sigmoid(score) * factor
        scaled = (slope * first.astype(F32)).astype(BF16)
        half = half + dot(scaled, second, ROWS)
    full = half + half.T
    quarter = width // 2
    upper = full[:quarter, :quarter]
    lower = full[quarter:, quarter:]
    i = lax.broadcasted_iota(jnp.int32, (quarter, quarter), 0)
    j = lax.broadcasted_iota(jnp.int32, (quarter, quarter), 1)
    diagonal = jnp.sum(jnp.where(i == j, lower, 0.0), axis=0, keepdims=True)
    corner = full[:quarter, quarter:].astype(BF16)
    mixed = jnp.where(i <= j, upper, lower).astype(BF16)
    extra = jnp.broadcast_to(diagonal, (PACK_EXTRA, quarter)).astype(BF16)
    for packed in outs:
        packed[pl.ds(0, quarter), :] = corner
        packed[pl.ds(quarter, quarter), :] = mixed
        packed[pl.ds(2 * quarter, PACK_EXTRA), :] = extra


def local_gradient(pieces, low, core, s, out):
    width = low.shape[1]
    quarter = width // 2
    i = lax.broadcasted_iota(jnp.int32, (quarter, quarter), 0)
    j = lax.broadcasted_iota(jnp.int32, (quarter, quarter), 1)
    x = lax.div(lax.axis_index("snap"), 2)
    piece = pieces[lax.rem(x - s + RING, RING)]
    corner = piece[:quarter]
    mixed = piece[quarter : 2 * quarter].astype(F32)
    diagonal = piece[2 * quarter :].astype(F32)[0:1]
    turned = mixed.T
    upper = jnp.where(i <= j, mixed, turned).astype(BF16)
    lower = jnp.where(i > j, mixed, jnp.where(i < j, turned, diagonal)).astype(BF16)
    whole = jnp.concatenate(
        [
            jnp.concatenate([upper, corner], axis=1),
            jnp.concatenate([corner.T, lower], axis=1),
        ],
        axis=0,
    )
    out[s] = dot(whole, low[2 * s + core])


def local_kernel(along, low, mine):
    core = lax.rem(lax.axis_index("snap"), 2)
    for s in range(mine.shape[0]):
        local_gradient(along, low, core, s, mine)


def backward_kernel(
    mine,
    other,
    keep,
    gate_slope,
    proposal_slope,
    reset_slope,
    reset,
    low,
    weights_wide,
    reset_wide,
    turned_high,
    turned_low,
    adjoint_rows,
    grads,
    initial_grad,
    adjoints,
    others,
):
    steps, width = low.shape[0], low.shape[1]
    place, node = lax.axis_index("snap"), lax.axis_index("node")
    core = lax.rem(place, 2)
    for s in range(steps // 2):
        local_gradient(other, low, 1 - core, s, others)

    def gate(k, parts):
        return dot3((turned_high[k], turned_low[k - 2]), parts)

    def gate_once(k, part):
        return dot(turned_high[k], part)

    grads[...] = jnp.zeros_like(grads)

    def step(t, local, carry):
        g = local + carry
        adjoints[t] = g
        d2 = g * proposal_slope[t]
        d2_parts = split(d2)
        mixed = gate(3, d2_parts)
        d0 = g * gate_slope[t]
        d0_high = d0.astype(BF16)
        fresh = g * keep[t] + (gate_once(0, d0_high) + gate(2, d2_parts))
        d1 = mixed * reset_slope[t]
        d1_high = d1.astype(BF16)
        fresh = fresh + mixed * reset[t] + gate_once(1, d1_high)
        lanes = pl.ds(pl.multiple_of(t * width, width), width)
        before = weights_wide[:, lanes]
        grads[0] += dot(d0_high, before, LANES)
        grads[1] += dot(d1_high, before, LANES)
        grads[2] += dot(d2_parts[0], before, LANES)
        grads[3] += dot(d2_parts[0], reset_wide[:, lanes], LANES)
        grads[4] += d0
        grads[5] += d1
        grads[6] += d2
        return fresh

    def steps_of_chips(turn, carry):
        for k in range(CHIPS_AT_ONCE):
            s = steps // 2 - 1 - (turn * CHIPS_AT_ONCE + k)
            carry = step(2 * s + 1, jnp.where(core == 1, mine[s], others[s]), carry)
            carry = step(2 * s, jnp.where(core == 0, mine[s], others[s]), carry)
        return carry

    turns = steps // (2 * CHIPS_AT_ONCE)
    initial_grad[...] = lax.fori_loop(0, turns, steps_of_chips, jnp.zeros((width, width), F32))
    share = adjoint_rows.shape[0]
    start = pl.multiple_of(node * share, share)
    adjoint_rows[...] = adjoints[place, pl.ds(start, share), :]


def params(megabytes):
    return pltpu.CompilerParams(vmem_limit_bytes=megabytes * 2**20)


VMEM = pl.BlockSpec(memory_space=pltpu.VMEM)
HBM = pl.BlockSpec(memory_space=pltpu.HBM)


def ring_parts(copies, axis, stride, count):
    size = lax.axis_size(axis)
    span = stride * count
    parts = []
    for turn in sorted(range(1, count), key=lambda k: -min(k, count - k)):
        route = [(i, i - i % span + (i % span + turn * stride) % span) for i in range(size)]
        parts.append(lax.ppermute(copies[turn], axis, route))
    return parts


def sum_kernel(own, first, second, third, *copies):
    total = (own[...].astype(F32) + first[...].astype(F32)) + (
        second[...].astype(F32) + third[...].astype(F32)
    )
    total = total.astype(BF16)
    for copy in copies:
        copy[...] = total


def ring_sum(copies, axis, stride, count):
    parts = ring_parts(copies, axis, stride, count)
    like = jax.ShapeDtypeStruct(copies[0].shape, BF16)
    return pl.pallas_call(
        sum_kernel,
        out_shape=[like] * RING,
        in_specs=[VMEM] * RING,
        out_specs=[VMEM] * RING,
        compiler_params=params(4),
        name="ring_sum",
    )(copies[0], *parts)


def body(
    features, tile_ids, tile_values, pos_edges, neg_edges, initial_weight, gate_mats, gate_bias
):
    snap_count = lax.axis_size("snap")
    node_count = lax.axis_size("node")
    own = features[0]
    rows, width = own.shape
    side = tile_values.shape[-1]
    square = (snap_count, width, width)

    sources = [
        pltpu.with_memory_space_constraint(array, pltpu.HBM)
        for array in (initial_weight, gate_mats, gate_bias)
    ]
    gate_scratch = [
        pltpu.VMEM((width, width), F32),
        pltpu.VMEM((4, width, width), F32),
        pltpu.VMEM((3, width, width), F32),
        pltpu.VMEM((4, width, width), BF16),
        pltpu.VMEM((4, width, width), BF16),
        pltpu.SemaphoreType.DMA((8,)),
    ]
    wide = jax.ShapeDtypeStruct(square, F32)
    flat = jax.ShapeDtypeStruct((width, width), BF16)
    before, early_score_matrix = pl.pallas_call(
        early_kernel,
        out_shape=[jax.ShapeDtypeStruct(((snap_count - 1) // STRIDE, width, width), F32), flat],
        in_specs=[HBM] * 3,
        out_specs=[VMEM] * 2,
        scratch_shapes=[pltpu.VMEM(square, BF16)] + gate_scratch,
        compiler_params=params(7),
        name="forward_early",
    )(*sources)
    sent, before = lax.optimization_barrier((own, before))
    even_pairs = [(i, i ^ 1) for i in range(node_count)]
    odd_pairs = [(i, (i - 1 + 2 * (i % 2)) % node_count) for i in range(node_count)]
    even_side = lax.ppermute(sent, "node", even_pairs)
    odd_side = lax.ppermute(sent, "node", odd_pairs)

    long = jax.ShapeDtypeStruct((width, snap_count * width), BF16)
    outs = [wide] * 5 + [jax.ShapeDtypeStruct(square, BF16), long, long]
    outs += [jax.ShapeDtypeStruct((k, width, width), BF16) for k in (4, 2)] + [flat]
    *states, score_matrix = pl.pallas_call(
        late_kernel,
        out_shape=outs,
        in_specs=[HBM] * 3 + [VMEM] * 2,
        out_specs=[VMEM] * len(outs),
        scratch_shapes=gate_scratch,
        compiler_params=params(7),
        name="forward_late",
    )(*sources, before, early_score_matrix)

    factor = float(rows * node_count) ** (-0.5)
    pack_rows = width + PACK_EXTRA
    copies = pl.pallas_call(
        functools.partial(edge_kernel, factor),
        out_shape=[jax.ShapeDtypeStruct((pack_rows, width // 2), BF16)] * RING,
        in_specs=[VMEM] * 8,
        out_specs=[VMEM] * RING,
        scratch_shapes=[
            pltpu.VMEM(((rows + 2 * HALO) // side, side, width), BF16),
            pltpu.VMEM((rows, width), BF16),
            pltpu.VMEM((4 * pos_edges.shape[-1], width), BF16),
        ],
        compiler_params=params(9),
        name="edge_products",
    )(
        tile_ids[0],
        own,
        even_side,
        odd_side,
        tile_values.reshape(-1, side, side),
        pos_edges[0],
        neg_edges[0],
        score_matrix,
    )

    copies = ring_sum(copies, "node", 1, RING)
    copies = ring_sum(copies, "node", RING, node_count // RING)
    far, near, back = ring_parts(copies, "snap", 2, snap_count // 2)
    along = jnp.stack([copies[0], near, far, back])
    other = lax.ppermute(along, "snap", [(i, i ^ 1) for i in range(snap_count)])

    half = (snap_count // 2, width, width)
    mine = pl.pallas_call(
        local_kernel,
        out_shape=jax.ShapeDtypeStruct(half, F32),
        in_specs=[VMEM] * 2,
        out_specs=VMEM,
        compiler_params=params(8),
        name="local_gradients",
    )(along, states[5])

    share = width // node_count
    adjoint_rows, grads, initial_grad = pl.pallas_call(
        backward_kernel,
        out_shape=[
            jax.ShapeDtypeStruct((share, width), F32),
            jax.ShapeDtypeStruct((7, width, width), F32),
            jax.ShapeDtypeStruct((width, width), F32),
        ],
        in_specs=[VMEM] * 12,
        out_specs=[VMEM] * 3,
        scratch_shapes=[pltpu.VMEM(square, F32), pltpu.VMEM(half, F32)],
        compiler_params=params(9),
        name="backward_chain",
    )(mine, other, *states)
    return adjoint_rows[None], grads, initial_grad


def solution(mesh):
    placed = (
        P("snap", "node", None),
        P("snap", "node", None),
        P("snap", "node", None, None, None),
        P("snap", None, "node"),
        P("snap", None, "node"),
        P(),
        P(),
        P(),
    )
    return jax.shard_map(
        body,
        mesh=mesh,
        in_specs=placed,
        out_specs=(P("snap", "node", None), P(), P()),
        check_vma=False,
    )
```

```python
import functools

import jax
import jax.numpy as jnp
from jax import lax
from jax.experimental import pallas as pl
from jax.experimental.pallas import tpu as pltpu
from jax.sharding import PartitionSpec as P

HALO = 1024
RING = 4
STRIDE = 3
CHIPS_AT_ONCE = 2
PACK_EXTRA = 16
F32 = jnp.float32
BF16 = jnp.bfloat16
INNER = (((1,), (0,)), ((), ()))
LANES = (((1,), (1,)), ((), ()))
ROWS = (((0,), (0,)), ((), ()))


def split(value):
    high = value.astype(BF16)
    return high, (value - high.astype(F32)).astype(BF16)


def dot(left, right, dims=INNER):
    return lax.dot_general(left, right, dims, preferred_element_type=F32)


def dot3(left, right, dims=INNER):
    return (
        dot(left[0], right[0], dims) + dot(left[0], right[1], dims) + dot(left[1], right[0], dims)
    )


def sigmoid(value):
    return 0.5 * jnp.tanh(0.5 * value) + 0.5


def load_gates(start_hbm, mats_hbm, bias_hbm, start, mats, bias, mats_high, mats_low, sems):
    copies = [pltpu.make_async_copy(start_hbm, start, sems.at[0])]
    copies += [
        pltpu.make_async_copy(mats_hbm.at[k], mats.at[k], sems.at[1 + k]) for k in range(4)
    ]
    copies += [
        pltpu.make_async_copy(bias_hbm.at[k], bias.at[k], sems.at[5 + k]) for k in range(3)
    ]
    for copy in copies:
        copy.start()
    copies[0].wait()
    for k in range(4):
        copies[1 + k].wait()
        mats_high[k], mats_low[k] = split(mats[k])
    for copy in copies[5:]:
        copy.wait()


def gate_step(weight, bias, mats_high, mats_low):
    def gate(k, parts):
        return dot3((mats_high[k], mats_low[k]), parts)

    parts = split(weight)
    r = sigmoid(gate(1, parts) + bias[1])
    mixed = r * weight
    mixed_parts = split(mixed)
    c_in = gate(2, parts)
    c_in = c_in + gate(3, mixed_parts)
    u_in = gate(0, parts)
    u = sigmoid(u_in + bias[0])
    c = jnp.tanh(c_in + bias[2])
    return u, r, c, mixed, (1.0 - u) * weight + u * c


def write_score_matrix(low, score_matrix):
    own = low[lax.axis_index("snap")]
    score_matrix[0], score_matrix[1] = split(dot(own, own, LANES))


def early_kernel(start_hbm, mats_hbm, bias_hbm, before, score_matrix, low, *scratch):
    start, mats, bias, mats_high, mats_low, sems = scratch

    @pl.when(lax.rem(lax.axis_index("snap"), 2) == 1)
    def _():
        load_gates(start_hbm, mats_hbm, bias_hbm, *scratch)
        weight = start[...]
        for t in range(low.shape[0]):
            if t > 0 and t % STRIDE == 0:
                before[t // STRIDE - 1] = weight
            weight = gate_step(weight, bias, mats_high, mats_low)[-1]
            low[t] = weight.astype(BF16)
        write_score_matrix(low, score_matrix)


def late_kernel(
    start_hbm,
    mats_hbm,
    bias_hbm,
    before,
    early_score_matrix,
    keep,
    gate_slope,
    proposal_slope,
    reset_slope,
    reset,
    low,
    weights_wide,
    reset_wide,
    turned_high,
    turned_low,
    score_matrix,
    *scratch,
):
    start, mats, bias, mats_high, mats_low, sems = scratch
    steps, width = low.shape[0], low.shape[1]
    odd = lax.rem(lax.axis_index("snap"), 2) == 1
    load_gates(start_hbm, mats_hbm, bias_hbm, *scratch)

    def record(t, weight):
        u, r, c, mixed, fresh = gate_step(weight, bias, mats_high, mats_low)
        keep[t] = 1.0 - u
        reset[t] = r
        gate_slope[t] = (c - weight) * (u * (1.0 - u))
        proposal_slope[t] = u * (1.0 - c * c)
        reset_slope[t] = mixed * (1.0 - r)
        lanes = pl.ds(t * width, width)
        weights_wide[:, lanes] = weight.astype(BF16)
        reset_wide[:, lanes] = mixed.astype(BF16)
        low[t] = fresh.astype(BF16)
        return fresh

    @pl.when(odd)
    def _():
        weights = [start[...]] + [before[k] for k in range(before.shape[0])]
        for s in range(STRIDE):
            for k in range(len(weights)):
                if k * STRIDE + s < steps:
                    weights[k] = record(k * STRIDE + s, weights[k])
        score_matrix[...] = early_score_matrix[...]

    @pl.when(jnp.logical_not(odd))
    def _():
        weight = start[...]
        for t in range(steps):
            weight = record(t, weight)
        write_score_matrix(low, score_matrix)

    for k in range(4):
        turned_high[k] = mats_high[k].T
    for k in range(2):
        turned_low[k] = mats_low[k + 2].T


def edge_kernel(
    factor,
    ids,
    own,
    even_side,
    odd_side,
    tiles,
    pos,
    neg,
    score_matrix,
    *refs,
):
    *outs, extended, aggregated, picked = refs
    rows, width = own.shape
    side = tiles.shape[1]
    blocks = rows // side
    per_block = ids.shape[1]
    picks = ids[...]
    node, ends = lax.axis_index("node"), lax.axis_size("node") - 1
    odd = lax.rem(node, 2)
    inside = (node > 0) & (node < ends)
    far = jnp.where(inside, odd_side[...], jnp.zeros_like(odd_side))
    extended[pl.ds(2 * blocks * (1 - odd), blocks)] = even_side[...].reshape(blocks, side, width)
    extended[pl.ds(blocks, blocks)] = own[...].reshape(blocks, side, width)
    extended[pl.ds(2 * blocks * odd, blocks)] = far.reshape(blocks, side, width)
    for b in range(blocks):
        total = jnp.zeros((side, width), F32)
        for k in range(0, per_block, 2):
            tile = jnp.concatenate([tiles[b * per_block + k], tiles[b * per_block + k + 1]], axis=1)
            source = jnp.concatenate([extended[picks[b, k]], extended[picks[b, k + 1]]], axis=0)
            total = total + dot(tile, source)
        aggregated[pl.ds(b * side, side), :] = total.astype(BF16)

    edges = pos.shape[1]
    chunk = 512
    lane = lax.broadcasted_iota(jnp.int32, (chunk, side), 1)
    for c in range(4 * edges // chunk):
        end, offset = divmod(c * chunk, edges)
        source = (pos, neg)[end // 2]
        turned = [
            jnp.broadcast_to(
                source[pl.ds(end % 2, 1), pl.ds(offset + part * side, side)], (side, side)
            ).T
            for part in range(chunk // side)
        ]
        index = jnp.concatenate(turned, axis=0)
        onehot = jnp.concatenate(
            [(index == lane + part * side).astype(F32).astype(BF16) for part in range(rows // side)],
            axis=1,
        )
        picked[pl.ds(c * chunk, chunk), :] = dot(onehot, aggregated[...]).astype(BF16)

    half = jnp.zeros((width, width), F32)
    for sign in (0, 1):
        for c in range(edges // chunk):
            first = picked[pl.ds(2 * sign * edges + c * chunk, chunk), :]
            second = picked[pl.ds((2 * sign + 1) * edges + c * chunk, chunk), :]
            ends = dot(first, score_matrix[0]) + dot(first, score_matrix[1])
            ends = ends * second.astype(F32)
            score = jnp.sum(ends, axis=1, keepdims=True) * (1.0 / width)
            if sign == 0:
                slope = sigmoid(-score) * (-factor)
            else:
                slope = sigmoid(score) * factor
            scaled = (slope * first.astype(F32)).astype(BF16)
            half = half + dot(scaled, second, ROWS)
    full = half + half.T
    quarter = width // 2
    upper = full[:quarter, :quarter]
    lower = full[quarter:, quarter:]
    i = lax.broadcasted_iota(jnp.int32, (quarter, quarter), 0)
    j = lax.broadcasted_iota(jnp.int32, (quarter, quarter), 1)
    diagonal = jnp.sum(jnp.where(i == j, lower, 0.0), axis=0, keepdims=True)
    corner = full[:quarter, quarter:].astype(BF16)
    mixed = jnp.where(i <= j, upper, lower).astype(BF16)
    extra = jnp.broadcast_to(diagonal, (PACK_EXTRA, quarter)).astype(BF16)
    for packed in outs:
        packed[pl.ds(0, quarter), :] = corner
        packed[pl.ds(quarter, quarter), :] = mixed
        packed[pl.ds(2 * quarter, PACK_EXTRA), :] = extra


def local_gradient(pieces, low, core, s, out):
    width = low.shape[1]
    quarter = width // 2
    i = lax.broadcasted_iota(jnp.int32, (quarter, quarter), 0)
    j = lax.broadcasted_iota(jnp.int32, (quarter, quarter), 1)
    x = lax.div(lax.axis_index("snap"), 2)
    piece = pieces[lax.rem(x - s + RING, RING)]
    corner = piece[:quarter]
    mixed = piece[quarter : 2 * quarter].astype(F32)
    diagonal = piece[2 * quarter :].astype(F32)[0:1]
    turned = mixed.T
    upper = jnp.where(i <= j, mixed, turned).astype(BF16)
    lower = jnp.where(i > j, mixed, jnp.where(i < j, turned, diagonal)).astype(BF16)
    whole = jnp.concatenate(
        [
            jnp.concatenate([upper, corner], axis=1),
            jnp.concatenate([corner.T, lower], axis=1),
        ],
        axis=0,
    )
    out[s] = dot(whole, low[2 * s + core])


def local_kernel(along, low, mine):
    core = lax.rem(lax.axis_index("snap"), 2)
    for s in range(mine.shape[0]):
        local_gradient(along, low, core, s, mine)


def backward_kernel(
    mine,
    other,
    keep,
    gate_slope,
    proposal_slope,
    reset_slope,
    reset,
    low,
    weights_wide,
    reset_wide,
    turned_high,
    turned_low,
    adjoint_rows,
    grads,
    initial_grad,
    adjoints,
    others,
):
    steps, width = low.shape[0], low.shape[1]
    place, node = lax.axis_index("snap"), lax.axis_index("node")
    core = lax.rem(place, 2)
    for s in range(steps // 2):
        local_gradient(other, low, 1 - core, s, others)

    def gate(k, parts):
        return dot3((turned_high[k], turned_low[k - 2]), parts)

    def gate_once(k, part):
        return dot(turned_high[k], part)

    grads[...] = jnp.zeros_like(grads)

    def step(t, local, carry):
        g = local + carry
        adjoints[t] = g
        d2 = g * proposal_slope[t]
        d2_parts = split(d2)
        mixed = gate(3, d2_parts)
        two = gate(2, d2_parts)
        d0 = g * gate_slope[t]
        d0_high = d0.astype(BF16)
        lanes = pl.ds(pl.multiple_of(t * width, width), width)
        before = weights_wide[:, lanes]
        grads[0] += dot(d0_high, before, LANES)
        grads[2] += dot(d2_parts[0], before, LANES)
        grads[3] += dot(d2_parts[0], reset_wide[:, lanes], LANES)
        d1 = mixed * reset_slope[t]
        d1_high = d1.astype(BF16)
        fresh = g * keep[t] + gate_once(0, d0_high) + two
        fresh = fresh + mixed * reset[t] + gate_once(1, d1_high)
        grads[1] += dot(d1_high, before, LANES)
        grads[4] += d0
        grads[5] += d1
        grads[6] += d2
        return fresh

    def steps_of_chips(turn, carry):
        for k in range(CHIPS_AT_ONCE):
            s = steps // 2 - 1 - (turn * CHIPS_AT_ONCE + k)
            carry = step(2 * s + 1, jnp.where(core == 1, mine[s], others[s]), carry)
            carry = step(2 * s, jnp.where(core == 0, mine[s], others[s]), carry)
        return carry

    turns = steps // (2 * CHIPS_AT_ONCE)
    initial_grad[...] = lax.fori_loop(0, turns, steps_of_chips, jnp.zeros((width, width), F32))
    share = adjoint_rows.shape[0]
    start = pl.multiple_of(node * share, share)
    adjoint_rows[...] = adjoints[place, pl.ds(start, share), :]


def params(megabytes):
    return pltpu.CompilerParams(vmem_limit_bytes=megabytes * 2**20)


VMEM = pl.BlockSpec(memory_space=pltpu.VMEM)
HBM = pl.BlockSpec(memory_space=pltpu.HBM)


def ring_parts(copies, axis, stride, count):
    size = lax.axis_size(axis)
    span = stride * count
    parts = []
    for turn in sorted(range(1, count), key=lambda k: -min(k, count - k)):
        route = [(i, i - i % span + (i % span + turn * stride) % span) for i in range(size)]
        parts.append(lax.ppermute(copies[turn], axis, route))
    return parts


def sum_kernel(own, first, second, third, *copies):
    total = (own[...].astype(F32) + first[...].astype(F32)) + (
        second[...].astype(F32) + third[...].astype(F32)
    )
    total = total.astype(BF16)
    for copy in copies:
        copy[...] = total


def ring_sum(copies, axis, stride, count):
    parts = ring_parts(copies, axis, stride, count)
    like = jax.ShapeDtypeStruct(copies[0].shape, BF16)
    return pl.pallas_call(
        sum_kernel,
        out_shape=[like] * RING,
        in_specs=[VMEM] * RING,
        out_specs=[VMEM] * RING,
        compiler_params=params(4),
        name="ring_sum",
    )(copies[0], *parts)


def body(
    features, tile_ids, tile_values, pos_edges, neg_edges, initial_weight, gate_mats, gate_bias
):
    snap_count = lax.axis_size("snap")
    node_count = lax.axis_size("node")
    own = features[0]
    rows, width = own.shape
    side = tile_values.shape[-1]
    square = (snap_count, width, width)

    sources = [
        pltpu.with_memory_space_constraint(array, pltpu.HBM)
        for array in (initial_weight, gate_mats, gate_bias)
    ]
    gate_scratch = [
        pltpu.VMEM((width, width), F32),
        pltpu.VMEM((4, width, width), F32),
        pltpu.VMEM((3, width, width), F32),
        pltpu.VMEM((4, width, width), BF16),
        pltpu.VMEM((4, width, width), BF16),
        pltpu.SemaphoreType.DMA((8,)),
    ]
    wide = jax.ShapeDtypeStruct(square, F32)
    flat = jax.ShapeDtypeStruct((2, width, width), BF16)
    before, early_score_matrix = pl.pallas_call(
        early_kernel,
        out_shape=[jax.ShapeDtypeStruct(((snap_count - 1) // STRIDE, width, width), F32), flat],
        in_specs=[HBM] * 3,
        out_specs=[VMEM] * 2,
        scratch_shapes=[pltpu.VMEM(square, BF16)] + gate_scratch,
        compiler_params=params(7),
        name="forward_early",
    )(*sources)
    sent, before = lax.optimization_barrier((own, before))
    even_pairs = [(i, i ^ 1) for i in range(node_count)]
    odd_pairs = [(i, (i - 1 + 2 * (i % 2)) % node_count) for i in range(node_count)]
    even_side = lax.ppermute(sent, "node", even_pairs)
    odd_side = lax.ppermute(sent, "node", odd_pairs)

    long = jax.ShapeDtypeStruct((width, snap_count * width), BF16)
    outs = [wide] * 5 + [jax.ShapeDtypeStruct(square, BF16), long, long]
    outs += [jax.ShapeDtypeStruct((k, width, width), BF16) for k in (4, 2)] + [flat]
    *states, score_matrix = pl.pallas_call(
        late_kernel,
        out_shape=outs,
        in_specs=[HBM] * 3 + [VMEM] * 2,
        out_specs=[VMEM] * len(outs),
        scratch_shapes=gate_scratch,
        compiler_params=params(7),
        name="forward_late",
    )(*sources, before, early_score_matrix)

    factor = float(rows * node_count) ** (-0.5)
    pack_rows = width + PACK_EXTRA
    copies = pl.pallas_call(
        functools.partial(edge_kernel, factor),
        out_shape=[jax.ShapeDtypeStruct((pack_rows, width // 2), BF16)] * RING,
        in_specs=[VMEM] * 8,
        out_specs=[VMEM] * RING,
        scratch_shapes=[
            pltpu.VMEM(((rows + 2 * HALO) // side, side, width), BF16),
            pltpu.VMEM((rows, width), BF16),
            pltpu.VMEM((4 * pos_edges.shape[-1], width), BF16),
        ],
        compiler_params=params(9),
        name="edge_products",
    )(
        tile_ids[0],
        own,
        even_side,
        odd_side,
        tile_values.reshape(-1, side, side),
        pos_edges[0],
        neg_edges[0],
        score_matrix,
    )

    copies = ring_sum(copies, "node", 1, RING)
    copies = ring_sum(copies, "node", RING, node_count // RING)
    far, near, back = ring_parts(copies, "snap", 2, snap_count // 2)
    along = jnp.stack([copies[0], near, far, back])
    other = lax.ppermute(along, "snap", [(i, i ^ 1) for i in range(snap_count)])

    half = (snap_count // 2, width, width)
    mine = pl.pallas_call(
        local_kernel,
        out_shape=jax.ShapeDtypeStruct(half, F32),
        in_specs=[VMEM] * 2,
        out_specs=VMEM,
        compiler_params=params(8),
        name="local_gradients",
    )(along, states[5])

    share = width // node_count
    adjoint_rows, grads, initial_grad = pl.pallas_call(
        backward_kernel,
        out_shape=[
            jax.ShapeDtypeStruct((share, width), F32),
            jax.ShapeDtypeStruct((7, width, width), F32),
            jax.ShapeDtypeStruct((width, width), F32),
        ],
        in_specs=[VMEM] * 12,
        out_specs=[VMEM] * 3,
        scratch_shapes=[pltpu.VMEM(square, F32), pltpu.VMEM(half, F32)],
        compiler_params=params(9),
        name="backward_chain",
    )(mine, other, *states)
    return adjoint_rows[None], grads, initial_grad


def solution(mesh):
    placed = (
        P("snap", "node", None),
        P("snap", "node", None),
        P("snap", "node", None, None, None),
        P("snap", None, "node"),
        P("snap", None, "node"),
        P(),
        P(),
        P(),
    )
    return jax.shard_map(
        body,
        mesh=mesh,
        in_specs=placed,
        out_specs=(P("snap", "node", None), P(), P()),
        check_vma=False,
    )
```

```python
import functools

import jax
import jax.numpy as jnp
from jax import lax
from jax.experimental import pallas as pl
from jax.experimental.pallas import tpu as pltpu
from jax.sharding import PartitionSpec as P

HALO = 1024
RING = 4
STRIDE = 3
CHIPS_AT_ONCE = 2
PACK_EXTRA = 16
F32 = jnp.float32
BF16 = jnp.bfloat16
INNER = (((1,), (0,)), ((), ()))
LANES = (((1,), (1,)), ((), ()))
ROWS = (((0,), (0,)), ((), ()))


def split(value):
    high = value.astype(BF16)
    return high, (value - high.astype(F32)).astype(BF16)


def dot(left, right, dims=INNER):
    return lax.dot_general(left, right, dims, preferred_element_type=F32)


def dot3(left, right, dims=INNER):
    return (
        dot(left[0], right[0], dims) + dot(left[0], right[1], dims) + dot(left[1], right[0], dims)
    )


def sigmoid(value):
    return 0.5 * jnp.tanh(0.5 * value) + 0.5


def load_gates(start_hbm, mats_hbm, bias_hbm, start, mats, bias, mats_high, mats_low, sems):
    copies = [pltpu.make_async_copy(start_hbm, start, sems.at[0])]
    copies += [
        pltpu.make_async_copy(mats_hbm.at[k], mats.at[k], sems.at[1 + k]) for k in range(4)
    ]
    copies += [
        pltpu.make_async_copy(bias_hbm.at[k], bias.at[k], sems.at[5 + k]) for k in range(3)
    ]
    for k in (0, 2, 6, 3, 4, 1, 5, 7):
        copies[k].start()
    copies[0].wait()

    def arrive(k):
        copies[1 + k].wait()
        mats_high[k], mats_low[k] = split(mats[k])
        if k < 3:
            copies[5 + k].wait()

    return arrive


def gate_step(weight, bias, mats_high, mats_low, arrive):
    def gate(k, parts):
        if arrive is not None:
            arrive(k)
        return dot3((mats_high[k], mats_low[k]), parts)

    parts = split(weight)
    r = sigmoid(gate(1, parts) + bias[1])
    mixed = r * weight
    mixed_parts = split(mixed)
    c_in = gate(2, parts)
    c_in = c_in + gate(3, mixed_parts)
    u_in = gate(0, parts)
    u = sigmoid(u_in + bias[0])
    c = jnp.tanh(c_in + bias[2])
    return u, r, c, mixed, (1.0 - u) * weight + u * c


def write_score_matrix(low, score_matrix):
    own = low[lax.axis_index("snap")]
    score_matrix[0], score_matrix[1] = split(dot(own, own, LANES))


def early_kernel(start_hbm, mats_hbm, bias_hbm, before, score_matrix, low, *scratch):
    start, mats, bias, mats_high, mats_low, sems = scratch

    @pl.when(lax.rem(lax.axis_index("snap"), 2) == 1)
    def _():
        arrive = load_gates(start_hbm, mats_hbm, bias_hbm, *scratch)
        weight = start[...]
        for t in range(low.shape[0]):
            if t > 0 and t % STRIDE == 0:
                before[t // STRIDE - 1] = weight
            weight = gate_step(weight, bias, mats_high, mats_low, arrive if t == 0 else None)[-1]
            low[t] = weight.astype(BF16)
        write_score_matrix(low, score_matrix)


def late_kernel(
    start_hbm,
    mats_hbm,
    bias_hbm,
    before,
    early_score_matrix,
    keep,
    gate_slope,
    proposal_slope,
    reset_slope,
    reset,
    low,
    weights_wide,
    reset_wide,
    turned_high,
    turned_low,
    score_matrix,
    *scratch,
):
    start, mats, bias, mats_high, mats_low, sems = scratch
    steps, width = low.shape[0], low.shape[1]
    odd = lax.rem(lax.axis_index("snap"), 2) == 1

    def record(t, weight, arrive):
        first = arrive if t == 0 else None
        u, r, c, mixed, fresh = gate_step(weight, bias, mats_high, mats_low, first)
        keep[t] = 1.0 - u
        reset[t] = r
        gate_slope[t] = (c - weight) * (u * (1.0 - u))
        proposal_slope[t] = u * (1.0 - c * c)
        reset_slope[t] = mixed * (1.0 - r)
        lanes = pl.ds(t * width, width)
        weights_wide[:, lanes] = weight.astype(BF16)
        reset_wide[:, lanes] = mixed.astype(BF16)
        low[t] = fresh.astype(BF16)
        return fresh

    @pl.when(odd)
    def _():
        arrive = load_gates(start_hbm, mats_hbm, bias_hbm, *scratch)
        weights = [start[...]] + [before[k] for k in range(before.shape[0])]
        for s in range(STRIDE):
            for k in range(len(weights)):
                if k * STRIDE + s < steps:
                    weights[k] = record(k * STRIDE + s, weights[k], arrive)
        score_matrix[...] = early_score_matrix[...]

    @pl.when(jnp.logical_not(odd))
    def _():
        arrive = load_gates(start_hbm, mats_hbm, bias_hbm, *scratch)
        weight = start[...]
        for t in range(steps):
            weight = record(t, weight, arrive)
        write_score_matrix(low, score_matrix)

    for k in range(4):
        turned_high[k] = mats_high[k].T
    for k in range(2):
        turned_low[k] = mats_low[k + 2].T


def edge_kernel(
    factor,
    ids,
    own,
    even_side,
    odd_side,
    tiles,
    pos,
    neg,
    score_matrix,
    *refs,
):
    *outs, extended, aggregated, picked = refs
    rows, width = own.shape
    side = tiles.shape[1]
    blocks = rows // side
    per_block = ids.shape[1]
    picks = ids[...]
    node, ends = lax.axis_index("node"), lax.axis_size("node") - 1
    odd = lax.rem(node, 2)
    inside = (node > 0) & (node < ends)
    far = jnp.where(inside, odd_side[...], jnp.zeros_like(odd_side))
    extended[pl.ds(2 * blocks * (1 - odd), blocks)] = even_side[...].reshape(blocks, side, width)
    extended[pl.ds(blocks, blocks)] = own[...].reshape(blocks, side, width)
    extended[pl.ds(2 * blocks * odd, blocks)] = far.reshape(blocks, side, width)
    for b in range(blocks):
        total = jnp.zeros((side, width), F32)
        for k in range(0, per_block, 2):
            tile = jnp.concatenate([tiles[b * per_block + k], tiles[b * per_block + k + 1]], axis=1)
            source = jnp.concatenate([extended[picks[b, k]], extended[picks[b, k + 1]]], axis=0)
            total = total + dot(tile, source)
        aggregated[pl.ds(b * side, side), :] = total.astype(BF16)

    edges = pos.shape[1]
    chunk = 512
    lane = lax.broadcasted_iota(jnp.int32, (chunk, side), 1)
    for c in range(4 * edges // chunk):
        end, offset = divmod(c * chunk, edges)
        source = (pos, neg)[end // 2]
        turned = [
            jnp.broadcast_to(
                source[pl.ds(end % 2, 1), pl.ds(offset + part * side, side)], (side, side)
            ).T
            for part in range(chunk // side)
        ]
        index = jnp.concatenate(turned, axis=0)
        onehot = jnp.concatenate(
            [(index == lane + part * side).astype(F32).astype(BF16) for part in range(rows // side)],
            axis=1,
        )
        picked[pl.ds(c * chunk, chunk), :] = dot(onehot, aggregated[...]).astype(BF16)

    half = jnp.zeros((width, width), F32)
    for sign in (0, 1):
        for c in range(edges // chunk):
            first = picked[pl.ds(2 * sign * edges + c * chunk, chunk), :]
            second = picked[pl.ds((2 * sign + 1) * edges + c * chunk, chunk), :]
            ends = dot(first, score_matrix[0]) + dot(first, score_matrix[1])
            ends = ends * second.astype(F32)
            score = jnp.sum(ends, axis=1, keepdims=True) * (1.0 / width)
            if sign == 0:
                slope = sigmoid(-score) * (-factor)
            else:
                slope = sigmoid(score) * factor
            scaled = (slope * first.astype(F32)).astype(BF16)
            half = half + dot(scaled, second, ROWS)
    full = half + half.T
    quarter = width // 2
    upper = full[:quarter, :quarter]
    lower = full[quarter:, quarter:]
    i = lax.broadcasted_iota(jnp.int32, (quarter, quarter), 0)
    j = lax.broadcasted_iota(jnp.int32, (quarter, quarter), 1)
    diagonal = jnp.sum(jnp.where(i == j, lower, 0.0), axis=0, keepdims=True)
    corner = full[:quarter, quarter:].astype(BF16)
    mixed = jnp.where(i <= j, upper, lower).astype(BF16)
    extra = jnp.broadcast_to(diagonal, (PACK_EXTRA, quarter)).astype(BF16)
    for packed in outs:
        packed[pl.ds(0, quarter), :] = corner
        packed[pl.ds(quarter, quarter), :] = mixed
        packed[pl.ds(2 * quarter, PACK_EXTRA), :] = extra


def local_gradient(pieces, low, core, s, out):
    width = low.shape[1]
    quarter = width // 2
    i = lax.broadcasted_iota(jnp.int32, (quarter, quarter), 0)
    j = lax.broadcasted_iota(jnp.int32, (quarter, quarter), 1)
    x = lax.div(lax.axis_index("snap"), 2)
    piece = pieces[lax.rem(x - s + RING, RING)]
    corner = piece[:quarter]
    mixed = piece[quarter : 2 * quarter].astype(F32)
    diagonal = piece[2 * quarter :].astype(F32)[0:1]
    turned = mixed.T
    upper = jnp.where(i <= j, mixed, turned).astype(BF16)
    lower = jnp.where(i > j, mixed, jnp.where(i < j, turned, diagonal)).astype(BF16)
    whole = jnp.concatenate(
        [
            jnp.concatenate([upper, corner], axis=1),
            jnp.concatenate([corner.T, lower], axis=1),
        ],
        axis=0,
    )
    out[s] = dot(whole, low[2 * s + core])


def local_kernel(along, low, mine):
    core = lax.rem(lax.axis_index("snap"), 2)
    for s in range(mine.shape[0]):
        local_gradient(along, low, core, s, mine)


def backward_kernel(
    mine,
    other,
    keep,
    gate_slope,
    proposal_slope,
    reset_slope,
    reset,
    low,
    weights_wide,
    reset_wide,
    turned_high,
    turned_low,
    adjoint_rows,
    grads,
    initial_grad,
    adjoints,
    others,
):
    steps, width = low.shape[0], low.shape[1]
    place, node = lax.axis_index("snap"), lax.axis_index("node")
    core = lax.rem(place, 2)
    for s in range(steps // 2):
        local_gradient(other, low, 1 - core, s, others)

    def gate(k, parts):
        return dot3((turned_high[k], turned_low[k - 2]), parts)

    def gate_once(k, part):
        return dot(turned_high[k], part)

    grads[...] = jnp.zeros_like(grads)

    def step(t, local, carry):
        g = local + carry
        adjoints[t] = g
        d2 = g * proposal_slope[t]
        d2_parts = split(d2)
        mixed = gate(3, d2_parts)
        two = gate(2, d2_parts)
        d0 = g * gate_slope[t]
        d0_high = d0.astype(BF16)
        lanes = pl.ds(pl.multiple_of(t * width, width), width)
        before = weights_wide[:, lanes]
        grads[0] += dot(d0_high, before, LANES)
        grads[2] += dot(d2_parts[0], before, LANES)
        grads[3] += dot(d2_parts[0], reset_wide[:, lanes], LANES)
        d1 = mixed * reset_slope[t]
        d1_high = d1.astype(BF16)
        fresh = g * keep[t] + gate_once(0, d0_high) + two
        fresh = fresh + mixed * reset[t] + gate_once(1, d1_high)
        grads[1] += dot(d1_high, before, LANES)
        grads[4] += d0
        grads[5] += d1
        grads[6] += d2
        return fresh

    def steps_of_chips(turn, carry):
        for k in range(CHIPS_AT_ONCE):
            s = steps // 2 - 1 - (turn * CHIPS_AT_ONCE + k)
            carry = step(2 * s + 1, jnp.where(core == 1, mine[s], others[s]), carry)
            carry = step(2 * s, jnp.where(core == 0, mine[s], others[s]), carry)
        return carry

    turns = steps // (2 * CHIPS_AT_ONCE)
    initial_grad[...] = lax.fori_loop(0, turns, steps_of_chips, jnp.zeros((width, width), F32))
    share = adjoint_rows.shape[0]
    start = pl.multiple_of(node * share, share)
    adjoint_rows[...] = adjoints[place, pl.ds(start, share), :]


def params(megabytes):
    return pltpu.CompilerParams(vmem_limit_bytes=megabytes * 2**20)


VMEM = pl.BlockSpec(memory_space=pltpu.VMEM)
HBM = pl.BlockSpec(memory_space=pltpu.HBM)


def ring_parts(copies, axis, stride, count):
    size = lax.axis_size(axis)
    span = stride * count
    parts = []
    for turn in sorted(range(1, count), key=lambda k: -min(k, count - k)):
        route = [(i, i - i % span + (i % span + turn * stride) % span) for i in range(size)]
        parts.append(lax.ppermute(copies[turn], axis, route))
    return parts


def sum_kernel(own, first, second, third, *copies):
    total = (own[...].astype(F32) + first[...].astype(F32)) + (
        second[...].astype(F32) + third[...].astype(F32)
    )
    total = total.astype(BF16)
    for copy in copies:
        copy[...] = total


def ring_sum(copies, axis, stride, count):
    parts = ring_parts(copies, axis, stride, count)
    like = jax.ShapeDtypeStruct(copies[0].shape, BF16)
    return pl.pallas_call(
        sum_kernel,
        out_shape=[like] * RING,
        in_specs=[VMEM] * RING,
        out_specs=[VMEM] * RING,
        compiler_params=params(4),
        name="ring_sum",
    )(copies[0], *parts)


def body(
    features, tile_ids, tile_values, pos_edges, neg_edges, initial_weight, gate_mats, gate_bias
):
    snap_count = lax.axis_size("snap")
    node_count = lax.axis_size("node")
    own = features[0]
    rows, width = own.shape
    side = tile_values.shape[-1]
    square = (snap_count, width, width)

    sources = [
        pltpu.with_memory_space_constraint(array, pltpu.HBM)
        for array in (initial_weight, gate_mats, gate_bias)
    ]
    gate_scratch = [
        pltpu.VMEM((width, width), F32),
        pltpu.VMEM((4, width, width), F32),
        pltpu.VMEM((3, width, width), F32),
        pltpu.VMEM((4, width, width), BF16),
        pltpu.VMEM((4, width, width), BF16),
        pltpu.SemaphoreType.DMA((8,)),
    ]
    wide = jax.ShapeDtypeStruct(square, F32)
    flat = jax.ShapeDtypeStruct((2, width, width), BF16)
    before, early_score_matrix = pl.pallas_call(
        early_kernel,
        out_shape=[jax.ShapeDtypeStruct(((snap_count - 1) // STRIDE, width, width), F32), flat],
        in_specs=[HBM] * 3,
        out_specs=[VMEM] * 2,
        scratch_shapes=[pltpu.VMEM(square, BF16)] + gate_scratch,
        compiler_params=params(7),
        name="forward_early",
    )(*sources)
    sent, before = lax.optimization_barrier((own, before))
    even_pairs = [(i, i ^ 1) for i in range(node_count)]
    odd_pairs = [(i, (i - 1 + 2 * (i % 2)) % node_count) for i in range(node_count)]
    even_side = lax.ppermute(sent, "node", even_pairs)
    odd_side = lax.ppermute(sent, "node", odd_pairs)

    long = jax.ShapeDtypeStruct((width, snap_count * width), BF16)
    outs = [wide] * 5 + [jax.ShapeDtypeStruct(square, BF16), long, long]
    outs += [jax.ShapeDtypeStruct((k, width, width), BF16) for k in (4, 2)] + [flat]
    *states, score_matrix = pl.pallas_call(
        late_kernel,
        out_shape=outs,
        in_specs=[HBM] * 3 + [VMEM] * 2,
        out_specs=[VMEM] * len(outs),
        scratch_shapes=gate_scratch,
        compiler_params=params(7),
        name="forward_late",
    )(*sources, before, early_score_matrix)

    factor = float(rows * node_count) ** (-0.5)
    pack_rows = width + PACK_EXTRA
    copies = pl.pallas_call(
        functools.partial(edge_kernel, factor),
        out_shape=[jax.ShapeDtypeStruct((pack_rows, width // 2), BF16)] * RING,
        in_specs=[VMEM] * 8,
        out_specs=[VMEM] * RING,
        scratch_shapes=[
            pltpu.VMEM(((rows + 2 * HALO) // side, side, width), BF16),
            pltpu.VMEM((rows, width), BF16),
            pltpu.VMEM((4 * pos_edges.shape[-1], width), BF16),
        ],
        compiler_params=params(9),
        name="edge_products",
    )(
        tile_ids[0],
        own,
        even_side,
        odd_side,
        tile_values.reshape(-1, side, side),
        pos_edges[0],
        neg_edges[0],
        score_matrix,
    )

    copies = ring_sum(copies, "node", 1, RING)
    copies = ring_sum(copies, "node", RING, node_count // RING)
    far, near, back = ring_parts(copies, "snap", 2, snap_count // 2)
    along = jnp.stack([copies[0], near, far, back])
    other = lax.ppermute(along, "snap", [(i, i ^ 1) for i in range(snap_count)])

    half = (snap_count // 2, width, width)
    mine = pl.pallas_call(
        local_kernel,
        out_shape=jax.ShapeDtypeStruct(half, F32),
        in_specs=[VMEM] * 2,
        out_specs=VMEM,
        compiler_params=params(8),
        name="local_gradients",
    )(along, states[5])

    share = width // node_count
    adjoint_rows, grads, initial_grad = pl.pallas_call(
        backward_kernel,
        out_shape=[
            jax.ShapeDtypeStruct((share, width), F32),
            jax.ShapeDtypeStruct((7, width, width), F32),
            jax.ShapeDtypeStruct((width, width), F32),
        ],
        in_specs=[VMEM] * 12,
        out_specs=[VMEM] * 3,
        scratch_shapes=[pltpu.VMEM(square, F32), pltpu.VMEM(half, F32)],
        compiler_params=params(9),
        name="backward_chain",
    )(mine, other, *states)
    return adjoint_rows[None], grads, initial_grad


def solution(mesh):
    placed = (
        P("snap", "node", None),
        P("snap", "node", None),
        P("snap", "node", None, None, None),
        P("snap", None, "node"),
        P("snap", None, "node"),
        P(),
        P(),
        P(),
    )
    return jax.shard_map(
        body,
        mesh=mesh,
        in_specs=placed,
        out_specs=(P("snap", "node", None), P(), P()),
        check_vma=False,
    )
```
